128 devices in a mesh: row: 16 (over y, x), col: 8 (over z, core).
Axes of the slice: x: 4, y: 4, z: 4, core: 2. Of those that a mesh axis runs over, the one named last changes fastest.
Arguments:
- offsets: float32 [3, 131072], P(None, ('row', 'col')), may hold values from 0 to 31.5
- measured: float32 [3, 131072], P(None, ('row', 'col')), may hold values from -6 to 6
- block_brick: int32 [1024], P(('row', 'col')), may hold values from 0 to 127
- block_count: int32 [1024], P(('row', 'col')), may hold values from 32 to 128, as said below
Outputs:
- vort_spec: float32 [2, 3, 32, 1024, 1024], P(None, None, 'col', 'row')
- residual: float32 [3, 131072], P(None, ('row', 'col'))
The draws below stay inside these ranges and needn't reach their ends.
Inputs may be any that keep to these rules, and one draw needn't show every extreme that they name: `block_brick`: brick of each block inside the x slab of the block's device row, numbered bx * 32 * 2 + by * 2 + bz. `block_count`: live slots are the first ones of a block; some block is full.
All inputs are finite; a program needn't handle non-finite values.
Results may differ from the reference program's by a relative error of at most 0.0003.
Values sent between devices are 32-bit elements; how exact they have to be, the bound alone decides.
No kernel may reach another device: no remote copies, remote signals or barrier semaphores. Data moves between devices by JAX's collectives and lax.ppermute only.
A program may use at most 192 MiB of HBM per device.

```python
import math
import jax
import jax.numpy as jnp
import numpy as np

NX = 1024
NY = 1024
NZ = 64
BRICK = 32
BLK = 8
ROWS = 131072
BLOCKS = 1024
BRICKS_ROW = 128
N_ROW = 16
N_COL = 8


def draw_block_count(key, part):
    key = jax.random.fold_in(key, 11)
    counts = jax.random.randint(key, (BLOCKS,), 32, 129)
    return counts.at[0].set(128)


def set_ends(array, stream_key, low, largest):
    dims = array.shape
    spot = [jax.random.randint(jax.random.fold_in(stream_key, axis), (), 0, dims[axis]) for axis in range(len(dims))]
    array = array.at[tuple(spot)].set(low)
    longest = dims.index(max(dims))
    spot[longest] = (spot[longest] + 1) % dims[longest]
    return array.at[tuple(spot)].set(largest)


def block_levels(own_key, shape, cuts, low, largest):
    gain = 1.0
    for axis_at, blocks in cuts:
        draws = jax.random.uniform(jax.random.fold_in(jax.random.fold_in(own_key, 6), axis_at), (blocks,), jnp.float32, low / len(cuts), largest / len(cuts))
        gain = gain * jnp.repeat(jnp.exp(draws), shape[axis_at] // blocks).reshape((-1,) + (1,) * (len(shape) - 1 - axis_at))
    return gain


def rank_table(amount, skew):
    portions = [(1 << 20) // math.isqrt(standing ** skew) + 1 for standing in range(1, amount + 1)]
    width = 1 + sum(portions) // (1 << 30)
    return np.cumsum(np.array([max(1, weight // width) for weight in portions]))


def ranked(key, extent, amount, slope):
    listing = rank_table(amount, slope)
    lot = jax.random.randint(jax.random.fold_in(key, 1), extent, 0, int(listing[amount - 1]))
    standing = jnp.searchsorted(jnp.asarray(listing, jnp.int32), lot, side="right")
    return jax.random.permutation(jax.random.fold_in(key, 2), amount)[standing].astype(jnp.int32)


def bell_draw(rng, dims, scale, limit, pieces=(), kind=jnp.bfloat16):
    drawn = jax.random.normal(rng, dims, jnp.float32) * scale
    if len(pieces) > 0:
        drawn = block_levels(rng, dims, pieces, -0.22, 0.18) * drawn
    return jnp.clip(drawn, min=-limit, max=limit).astype(kind)


def setup_inputs(seed: int = 0) -> dict:
    key_list = jax.random.split(jax.random.key(seed), 5)
    return {
        "offsets": jnp.clip(31.5 * jax.random.uniform(key_list[0], (3, ROWS), jnp.float32) ** block_levels(key_list[0], (3, ROWS), ((1, 128),), -0.2, 0.2), 0.0, 31.5),
        "measured": bell_draw(key_list[1], (3, ROWS), 1.0, 6.0, ((1, 128),), jnp.float32),
        "block_brick": set_ends(ranked(key_list[2], (BLOCKS,), BRICKS_ROW, 2), jax.random.fold_in(key_list[2], 3), 0, BRICKS_ROW - 1).astype(jnp.int32),
        "block_count": draw_block_count(jax.random.fold_in(key_list[4], 71), 0),
    }


TWO_PI = 2.0 * math.pi

def wavenumber(index, length, dtype):
    signed = jnp.where(index < length // 2, index, index - length)
    return TWO_PI * signed.astype(dtype) / length

def position_order(length):
    position = jnp.arange(length, dtype=jnp.int32)
    return (position % 128 * (length // 128) + position // 128).astype(jnp.int32)

def reference(offsets, measured, block_brick, block_count):
    dtype = offsets.dtype
    total_rows = offsets.shape[1]
    slots = BLK * 128
    planes = NX // N_ROW
    modes = NZ // 2
    cells = NX * NY * NZ
    slot_index = jnp.arange(total_rows, dtype=jnp.int32)
    block = slot_index // 128
    brick = block_brick[block]
    count = block_count[block]
    live = (slot_index % 128 < count).astype(dtype)
    slab = slot_index // slots // N_COL
    bricks_y = NY // BRICK
    bricks_z = NZ // BRICK
    brick_x = brick // (bricks_y * bricks_z)
    brick_y = brick // bricks_z % bricks_y
    brick_z = brick % bricks_z
    lower = jnp.floor(offsets)
    fraction = offsets - lower
    cell = lower.astype(jnp.int32)
    cell_x = slab * planes + BRICK * brick_x + cell[0]
    cell_y = BRICK * brick_y + cell[1]
    cell_z = BRICK * brick_z + cell[2]
    xs_pair = [cell_x % NX, (cell_x + 1) % NX]
    ys_pair = [cell_y % NY, (cell_y + 1) % NY]
    zs_pair = [cell_z % NZ, (cell_z + 1) % NZ]
    wx_pair = [1.0 - fraction[0], fraction[0]]
    wy_pair = [1.0 - fraction[1], fraction[1]]
    wz_pair = [1.0 - fraction[2], fraction[2]]
    corners = []
    for first in range(2):
        for second in range(2):
            for third in range(2):
                corners.append((xs_pair[first], ys_pair[second], zs_pair[third], wx_pair[first] * wy_pair[second] * wz_pair[third]))

    def interpolate(field):
        result = jnp.zeros((3, total_rows), dtype)
        for point_x, point_y, point_z, weight in corners:
            result = result + field[:, point_x, point_y, point_z] * weight[None]
        return result

    def spread(values):
        field = jnp.zeros((3, NX, NY, NZ), dtype)
        for point_x, point_y, point_z, weight in corners:
            field = field.at[:, point_x, point_y, point_z].add(values * weight[None])
        return field
    index_x = jnp.arange(NX, dtype=jnp.int32)
    index_y = jnp.arange(NY, dtype=jnp.int32)
    index_z = jnp.arange(modes, dtype=jnp.int32)
    wave_x = wavenumber(index_x, NX, dtype)[:, None, None]
    wave_y = wavenumber(index_y, NY, dtype)[None, :, None]
    wave_z = (TWO_PI * index_z.astype(dtype) / NZ)[None, None, :]
    valid = (index_x != NX // 2)[:, None, None] & (index_y != NY // 2)[None, :, None]
    anchor = (index_x == 0)[:, None, None] & (index_y == 0)[None, :, None] & (index_z == 0)[None, None, :]
    valid = valid & jnp.logical_not(anchor)
    squared = wave_x * wave_x + wave_y * wave_y + wave_z * wave_z
    inverse = jnp.where(valid, 1.0 / jnp.where(valid, squared, 1.0), 0.0)

    def biot_savart(spectrum):
        crossed = jnp.stack([wave_y * spectrum[2] - wave_z * spectrum[1], wave_z * spectrum[0] - wave_x * spectrum[2], wave_x * spectrum[1] - wave_y * spectrum[0]])
        return 1j * crossed * inverse[None]

    def forward(values):
        return biot_savart(jnp.fft.rfftn(spread(values), axes=(1, 2, 3))[..., :modes])

    def at_points(spectrum):
        padded = jnp.concatenate([spectrum, jnp.zeros(spectrum.shape[:3] + (1,), spectrum.dtype)], 3)
        return interpolate(jnp.fft.irfftn(padded, s=(NX, NY, NZ), axes=(1, 2, 3)))
    mode_weight = (jnp.where(index_z == 0, 1.0, 2.0).astype(dtype) / cells)[None, None, None, :]

    def spectral_norm(spectrum):
        return jnp.sum(mode_weight * (spectrum.real * spectrum.real + spectrum.imag * spectrum.imag))
    residual = measured * live[None]
    gradient = forward(residual)
    gamma = spectral_norm(gradient)
    velocity = at_points(biot_savart(gradient))
    curvature = jnp.sum(velocity * velocity * live[None])
    step_length = gamma / curvature
    vorticity = step_length * gradient
    residual = residual - step_length * velocity * live[None]
    scaled = vorticity / math.sqrt(cells)
    natural = jnp.stack([scaled.real, scaled.imag]).transpose(0, 1, 4, 3, 2)
    natural = jnp.take(natural, position_order(NY), axis=3)
    natural = jnp.take(natural, position_order(NX), axis=4)
    return (natural.astype(jnp.float32), residual.astype(jnp.float32))
```

```python
import math

import jax
import jax.numpy as jnp
import ml_dtypes
import numpy as np
from jax import lax
from jax.experimental import pallas as pl
from jax.experimental.pallas import tpu as pltpu
from jax.sharding import PartitionSpec as P

NX = 1024
NY = 1024
NZ = 64
CELLS = float(NX * NY * NZ)
TWO_PI = 2.0 * math.pi
F32 = jnp.float32
BF16 = jnp.bfloat16
VMEM_LIMIT = 56 * 1024 * 1024
VMEM = pl.BlockSpec(memory_space=pltpu.VMEM)
SMEM = pl.BlockSpec(memory_space=pltpu.SMEM)


def halves(table):
    table = table.astype(np.float32)
    high = table.astype(ml_dtypes.bfloat16)
    low = (table - high.astype(np.float32)).astype(ml_dtypes.bfloat16)
    return np.stack([high, low])


def table_y():
    first = np.arange(8)[:, None, None]
    angle = TWO_PI * ((np.arange(128)[None, :, None] * 8 + first) * np.arange(128)[None, None, :] % 1024) / 1024
    cosine, sine = np.cos(angle), np.sin(angle)
    return np.concatenate([np.concatenate([cosine, sine], 2), np.concatenate([-sine, cosine], 2)], 1)


def table_x():
    result = np.zeros((8, 2, 2, 64, 2, 64, 2))
    inner = np.arange(64)
    for first in range(8):
        for upper in range(2):
            wave = 16 * np.arange(64) + first + 8 * upper
            angle = TWO_PI * (inner[:, None] * wave[None, :] % 1024) / 1024
            result[first, upper, 0, :, 0, :, upper] = np.cos(angle)
            result[first, upper, 1, :, 0, :, upper] = np.sin(angle)
            result[first, upper, 0, :, 1, :, upper] = -np.sin(angle)
            result[first, upper, 1, :, 1, :, upper] = np.cos(angle)
    return result.reshape(8, 256, 256)


def split(value):
    high = value.astype(BF16)
    return high, (value - high.astype(F32)).astype(BF16)


def mul(left, right):
    return jnp.dot(left, right, preferred_element_type=F32)


def mul_t(left, right):
    return lax.dot_general(left, right, (((1,), (1,)), ((), ())), preferred_element_type=F32)


def small_dft(values, sign):
    count = len(values)
    if count == 1:
        return values
    even = small_dft(values[0::2], sign)
    odd = small_dft(values[1::2], sign)
    low, high = [], []
    for k in range(count // 2):
        real, imag = odd[k]
        if k > 0:
            if 4 * k == count:
                real, imag = (-imag, real) if sign > 0 else (imag, -real)
            elif 8 * k == count:
                root = math.sqrt(0.5)
                if sign > 0:
                    real, imag = (real - imag) * root, (real + imag) * root
                else:
                    real, imag = (real + imag) * root, (imag - real) * root
            elif 8 * k == 3 * count:
                root = math.sqrt(0.5)
                if sign > 0:
                    real, imag = (real + imag) * -root, (real - imag) * root
                else:
                    real, imag = (imag - real) * root, (real + imag) * -root
            else:
                cosine = math.cos(TWO_PI * k / count)
                sine = sign * math.sin(TWO_PI * k / count)
                real, imag = real * cosine - imag * sine, real * sine + imag * cosine
        low.append((even[k][0] + real, even[k][1] + imag))
        high.append((even[k][0] - real, even[k][1] - imag))
    return low + high


def hat(distance):
    return jnp.maximum(1.0 - jnp.abs(distance), 0.0)


def ramp(shape, axis):
    return lax.broadcasted_iota(jnp.int32, shape, axis).astype(F32)


def brick_place(brick):
    return brick // 64, brick // 2 % 32, brick % 2


def block_points(points, block):
    lane = pl.multiple_of(block % 8 * 128, 128)
    return points[block // 8, :, pl.ds(lane, 128)]


def depth_wave(points, meta, depth):
    index = lax.broadcasted_iota(jnp.int32, (8, 128), 0)
    mode = 4 * meta[65] + 2 * (index // 4) + index % 2
    turn = 16 * (index // 2 % 2)

    def wave(cell):
        angle = (mode * cell + turn) & 63
        value = (jnp.abs(angle - 32) - 16).astype(F32) * (math.pi / 32.0)
        square = value * value
        total = -1.0 / 39916800.0
        for factor in (1.0 / 362880.0, -1.0 / 5040.0, 1.0 / 120.0, -1.0 / 6.0, 1.0):
            total = total * square + factor
        return total * value

    def step(block, carry):
        height = block_points(points, block)[2:3]
        lower = jnp.floor(height)
        part = height - lower
        cell = lower.astype(jnp.int32) + 32 * (meta[block] % 2)
        depth[block] = (1.0 - part) * wave(cell) + part * wave(cell + 1)
        return carry

    lax.fori_loop(0, 64, step, 0, unroll=4)


def edge_kernel(meta, points, depth, edge):
    depth_wave(points, meta, depth)
    edge[...] = jnp.zeros_like(edge)
    cells = ramp((256, 128), 0)

    def step(block, carry):
        place_x, place_y, _ = brick_place(meta[block])

        @pl.when(place_x == 1)
        def _():
            point = block_points(points, block)
            across = jnp.maximum(point[0:1] - 31.0, 0.0)
            waves = depth[block] * across
            source = jnp.concatenate([waves * point[3 + c : 4 + c] for c in range(3)], 0)
            weight = hat(cells - (32 * (place_y % 4)).astype(F32) - point[1:2])
            source_high, source_low = split(source)
            weight_high, weight_low = split(weight)
            value = (
                mul_t(source_high, weight_high) + mul_t(source_low, weight_high) + mul_t(source_high, weight_low)
            )
            lane = pl.multiple_of(place_y // 4 * 128, 128)
            edge[:, pl.ds(lane, 256)] += value

        return carry

    lax.fori_loop(0, 64, step, 0)
    edge[:, 0:128] += edge[:, 1024:1152]


def slab_weights(point, waves, place_x):
    across = hat(ramp((64, 128), 0) - (32 * place_x).astype(F32) - point[0:1])
    return jnp.concatenate([waves[i : i + 1] * across for i in range(8)], 0)


def spread_kernel(meta, points, depth, edge, table, out, field, parts):
    field[...] = jnp.zeros_like(field)

    def step(block, carry):
        place_x, place_y, _ = brick_place(meta[block])
        point = block_points(points, block)
        weight_high, weight_low = split(slab_weights(point, depth[block], place_x))
        along = hat(ramp((40, 128), 0) - point[1:2])
        source = jnp.concatenate([along * point[3 + c : 4 + c] for c in range(3)], 0)
        source_high, source_low = split(source)
        both = mul_t(jnp.concatenate([source_high, source_low], 0), weight_high)
        value = both[:120] + both[120:] + mul_t(source_high, weight_low)
        row = pl.multiple_of(place_y * 32, 32)
        for c in range(3):
            field[c, pl.ds(row, 40), :] += value[40 * c : 40 * c + 40]
        return carry

    lax.fori_loop(0, 64, step, 0, unroll=2)
    lane = lax.broadcasted_iota(jnp.int32, (16, 512), 1)
    place = (lane == 64 * (lax.broadcasted_iota(jnp.int32, (16, 512), 0) % 8)).astype(BF16)
    for c in range(3):
        field[c, 0:1, :] += field[c, 1024:1025, :]
        high, low = split(edge[8 * c : 8 * c + 8, :])
        columns = jnp.concatenate([high.astype(F32), low.astype(F32)], 0).T.astype(BF16)
        field[c, 0:1024, :] += mul(columns, place)

    def outer(tile, carry):
        row = pl.multiple_of(tile * 8, 8)
        for c in range(3):
            for p in range(2):
                lane = 256 * p
                values = [
                    (
                        field[c, pl.ds(128 * a + row, 8), lane : lane + 128],
                        field[c, pl.ds(128 * a + row, 8), lane + 128 : lane + 256],
                    )
                    for a in range(8)
                ]
                for k, (real, imag) in enumerate(small_dft(values, -1)):
                    at = 128 * (2 * c + p)
                    parts[k, pl.ds(row, 8), at : at + 128] = real
                    parts[k, pl.ds(128 + row, 8), at : at + 128] = imag
        return carry

    lax.fori_loop(0, 16, outer, 0)

    def inner(k, carry):
        high, low = split(parts[k])
        value = mul(table[0, k], high) + mul(table[1, k], high) + mul(table[0, k], low)
        for half in range(2):
            for p in range(2):
                for c in range(3):
                    for part in range(2):
                        row = 128 * part + 64 * half
                        at = 128 * (2 * c + p)
                        out[2 * k + half, p, c, part] = value[row : row + 64, at : at + 128]
        return carry

    lax.fori_loop(0, 8, inner, 0)


def spectrum_kernel(meta, received, table, table_back, spectrum, out, norm, parts, back):
    pair = pl.program_id(0)
    row = meta[64]
    lane = lax.broadcasted_iota(jnp.int32, (8, 128), 1)
    lower = lane < 64

    def turned(value):
        return pltpu.roll(value, 64, 1)

    def outer(tile, carry):
        at = pl.multiple_of(tile * 8, 8)
        for c in range(3):
            values = [
                (received[s, 0, c, 0, pl.ds(at, 8), :], received[s, 0, c, 1, pl.ds(at, 8), :]) for s in range(16)
            ]
            for k, (real, imag) in enumerate(small_dft(values, -1)):
                to = 128 * (k // 8)
                parts[k % 8, pl.ds(128 * c + at, 8), to : to + 128] = jnp.where(lower, real, turned(imag))
                parts[k % 8, pl.ds(128 * c + 64 + at, 8), to : to + 128] = jnp.where(lower, turned(real), imag)
        return carry

    lax.fori_loop(0, 8, outer, 0)

    index_y = 8 * (64 * (row % 2) + lax.broadcasted_iota(jnp.int32, (64, 128), 0)) + row // 2
    lane_x = lax.broadcasted_iota(jnp.int32, (64, 128), 1)
    wave_y = jnp.where(index_y < NY // 2, index_y, index_y - NY).astype(F32) * (TWO_PI / NY)

    def inner(k, total):
        high, low = split(parts[k])
        value = mul(high, table[0, k]) + mul(low, table[0, k]) + mul(high, table[1, k])
        index_x = 8 * lane_x + k
        wave_x = jnp.where(index_x < NX // 2, index_x, index_x - NX).astype(F32) * (TWO_PI / NX)
        flat = wave_x * wave_x + wave_y * wave_y
        valid = (index_y != NY // 2) & (index_x != NX // 2)
        to = pl.multiple_of(k * 128, 128)
        rows = [[None, None] for _ in range(3)]
        for h in range(2):
            index_z = 4 * meta[65] + 2 * pair + h
            wave_z = index_z.astype(F32) * (TWO_PI / NZ)
            weight = jnp.where(index_z == 0, 1.0, 2.0).astype(F32) / CELLS
            squared = flat + wave_z * wave_z
            keep = valid & (squared > 0.0)
            inverse = jnp.where(keep, 1.0 / jnp.where(keep, squared, 1.0), 0.0)

            def crossed(vector, scale):
                return [
                    (wave_y * vector[2] - wave_z * vector[1]) * scale,
                    (wave_z * vector[0] - wave_x * vector[2]) * scale,
                    (wave_x * vector[1] - wave_y * vector[0]) * scale,
                ]

            start = [128 * c + 64 * h for c in range(3)]
            real = [value[s : s + 64, 0:128] for s in start]
            imag = [value[s : s + 64, 128:256] for s in start]
            grad_real = crossed(imag, -inverse)
            grad_imag = crossed(real, inverse)
            square = 0.0
            for c in range(3):
                spectrum[0, c, h, :, pl.ds(to, 128)] = grad_real[c]
                spectrum[1, c, h, :, pl.ds(to, 128)] = grad_imag[c]
                square = square + grad_real[c] * grad_real[c] + grad_imag[c] * grad_imag[c]
            total = total + weight * square
            scale = inverse * weight
            back_real = crossed(grad_imag, -scale)
            back_imag = crossed(grad_real, scale)
            for c in range(3):
                rows[c][h] = jnp.concatenate([back_real[c], back_imag[c]], 1)
        high, low = split(jnp.concatenate([rows[c][h] for c in range(3) for h in range(2)], 0))
        back[k] = mul(high, table_back[0, k]) + mul(low, table_back[0, k]) + mul(high, table_back[1, k])
        return total

    total = lax.fori_loop(0, 8, inner, jnp.zeros((64, 128), F32))
    norm[0] = jnp.sum(total.reshape(8, 8, 128), axis=0)

    def last(tile, carry):
        at = pl.multiple_of(tile * 8, 8)
        for c in range(3):
            values = []
            for k in range(16):
                to = 128 * (k // 8)
                first = back[k % 8, pl.ds(128 * c + at, 8), to : to + 128]
                second = back[k % 8, pl.ds(128 * c + 64 + at, 8), to : to + 128]
                values.append((jnp.where(lower, first, turned(second)), jnp.where(lower, turned(first), second)))
            for s, (real, imag) in enumerate(small_dft(values, 1)):
                out[s, 0, c, 0, pl.ds(at, 8), :] = real
                out[s, 0, c, 1, pl.ds(at, 8), :] = imag
        return carry

    lax.fori_loop(0, 8, last, 0)


def gather_kernel(meta, points, depth, received, table, out, edge, field_high, field_low, parts):
    def inner(k, carry):
        columns = []
        for c in range(3):
            for p in range(2):
                columns.append(
                    jnp.concatenate(
                        [received[2 * k + half, p, c, part] for part in range(2) for half in range(2)], 0
                    )
                )
        high, low = split(jnp.concatenate(columns, 1))
        parts[k] = mul(table[0, k], high) + mul(table[1, k], high) + mul(table[0, k], low)
        return carry

    lax.fori_loop(0, 8, inner, 0)

    def outer(tile, carry):
        row = pl.multiple_of(tile * 16, 16)
        for c in range(3):
            for p in range(2):
                at = 128 * (2 * c + p)
                values = [
                    (parts[k, pl.ds(row, 16), at : at + 128], parts[k, pl.ds(128 + row, 16), at : at + 128])
                    for k in range(8)
                ]
                for a, pieces in enumerate(small_dft(values, 1)):
                    for part in range(2):
                        high, low = split(pieces[part])
                        lane = 256 * p + 128 * part
                        field_high[c, pl.ds(128 * a + row, 16), lane : lane + 128] = high
                        field_low[c, pl.ds(128 * a + row, 16), lane : lane + 128] = low
        return carry

    lax.fori_loop(0, 8, outer, 0)
    lane = lax.broadcasted_iota(jnp.int32, (16, 512), 1)
    place = (lane == 64 * lax.broadcasted_iota(jnp.int32, (16, 512), 0)).astype(BF16)
    for c in range(3):
        value = mul_t(place, field_high[c, 0:1024, :]) + mul_t(place, field_low[c, 0:1024, :])
        edge[8 * c : 8 * c + 8, :] = value[0:8]
        field_high[c, 1024:1040, :] = field_high[c, 0:16, :]
        field_low[c, 1024:1040, :] = field_low[c, 0:16, :]

    def step(block, carry):
        place_x, place_y, _ = brick_place(meta[block])
        point = block_points(points, block)
        weight_high, weight_low = split(slab_weights(point, depth[block], place_x))
        weights = jnp.concatenate([weight_high, weight_low], 1)
        along = hat(ramp((48, 128), 0) - point[1:2])
        row = pl.multiple_of(place_y * 32, 32)
        high = jnp.concatenate([field_high[c, pl.ds(row, 48), :] for c in range(3)], 0)
        low = jnp.concatenate([field_low[c, pl.ds(row, 48), :] for c in range(3)], 0)
        both = mul(high, weights)
        value = both[:, :128] + both[:, 128:] + mul(low, weight_high)
        for c in range(3):
            velocity = jnp.sum(along * value[48 * c : 48 * c + 48], axis=0, keepdims=True)
            out[block // 8, pl.ds(8 * c + block % 8, 1), :] = velocity
        return carry

    lax.fori_loop(0, 64, step, 0, unroll=2)


def border_kernel(meta, points, depth, edge, velocity, out, wide):
    out[...] = velocity[...]
    wide[:, 0:1024] = edge[...]
    wide[:, 1024:1152] = edge[:, 0:128]
    cells = ramp((256, 128), 0)

    def step(block, carry):
        place_x, place_y, _ = brick_place(meta[block])

        @pl.when(place_x == 1)
        def _():
            point = block_points(points, block)
            waves = depth[block] * jnp.maximum(point[0:1] - 31.0, 0.0)
            weight_high, weight_low = split(hat(cells - (32 * (place_y % 4)).astype(F32) - point[1:2]))
            lane = pl.multiple_of(place_y // 4 * 128, 128)
            high, low = split(wide[:, pl.ds(lane, 256)])
            value = mul(high, weight_high) + mul(low, weight_high) + mul(high, weight_low)
            for c in range(3):
                more = jnp.sum(waves * value[8 * c : 8 * c + 8], axis=0, keepdims=True)
                out[block // 8, pl.ds(8 * c + block % 8, 1), :] += more

        return carry

    lax.fori_loop(0, 64, step, 0)


def call(kernel, outs, specs, scratch=(), flops=0, traffic=0, **extra):
    return pl.pallas_call(
        kernel,
        out_shape=outs,
        in_specs=specs,
        scratch_shapes=list(scratch),
        cost_estimate=pl.CostEstimate(flops=flops, bytes_accessed=traffic, transcendentals=0),
        compiler_params=pltpu.CompilerParams(vmem_limit_bytes=VMEM_LIMIT),
        **extra,
    )


def shape(*dims):
    return jax.ShapeDtypeStruct(dims, F32)


def shifted(value, axis, steps):
    count = lax.axis_size(axis)
    return lax.ppermute(value, axis, [(source, (source + steps) % count) for source in range(count)])


def spread_out(value, axis):
    count = lax.axis_size(axis)
    return lax.all_to_all(jnp.broadcast_to(value[None], (count,) + value.shape), axis, 0, 0, tiled=True)


def exchange(value):
    return lax.all_to_all(value, "row", 0, 0, tiled=True)


def body(offsets, measured, block_brick, block_count):
    row = lax.axis_index("row")
    col = lax.axis_index("col")
    slot = jnp.arange(1024, dtype=jnp.int32) % 128
    live = (slot < jnp.repeat(block_count, 128)).astype(F32)
    residual = measured * live[None]
    bricks = jnp.repeat(block_brick, 128).astype(F32)[None]
    points = spread_out(jnp.concatenate([offsets, residual, bricks, bricks], 0), "col")
    bricks = points[:, 6, ::128].reshape(64).astype(jnp.int32)
    meta = jnp.concatenate([bricks, jnp.stack([row, col]).astype(jnp.int32)])
    y_table = table_y()
    x_table = table_x()
    forward_y = jnp.asarray(halves(y_table))
    inverse_y = jnp.asarray(halves(y_table.transpose(0, 2, 1)))
    forward_x = jnp.asarray(halves(x_table))
    inverse_x = jnp.asarray(halves(x_table.transpose(0, 2, 1)))

    depth, edge = call(edge_kernel, (shape(64, 8, 128), shape(24, 1152)), [SMEM, VMEM])(meta, points)
    edge = shifted(edge[:, :1024], "row", 1)
    sent = call(
        spread_kernel,
        shape(16, 2, 3, 2, 64, 128),
        [SMEM, VMEM, VMEM, VMEM, VMEM],
        [pltpu.VMEM((3, 1032, 512), F32), pltpu.VMEM((8, 256, 768), F32)],
    )(meta, points, depth, edge, forward_y)
    received = exchange(sent)
    block = (16, 1, 3, 2, 64, 128)
    spectrum, sent, norm = pl.pallas_call(
        spectrum_kernel,
        grid=(2,),
        out_shape=(shape(2, 3, 4, 64, 1024), shape(16, 2, 3, 2, 64, 128), shape(2, 8, 128)),
        in_specs=[
            SMEM,
            pl.BlockSpec(block, lambda i: (0, i, 0, 0, 0, 0)),
            VMEM,
            VMEM,
        ],
        out_specs=(
            pl.BlockSpec((2, 3, 2, 64, 1024), lambda i: (0, 0, i, 0, 0)),
            pl.BlockSpec(block, lambda i: (0, i, 0, 0, 0, 0)),
            pl.BlockSpec((1, 8, 128), lambda i: (i, 0, 0)),
        ),
        scratch_shapes=[pltpu.VMEM((8, 384, 256), F32), pltpu.VMEM((8, 384, 256), F32)],
        compiler_params=pltpu.CompilerParams(vmem_limit_bytes=VMEM_LIMIT),
    )(meta, received, forward_x, inverse_x)
    received = exchange(sent)
    velocity, edge = call(
        gather_kernel,
        (shape(8, 24, 128), shape(24, 1024)),
        [SMEM, VMEM, VMEM, VMEM, VMEM],
        [pltpu.VMEM((3, 1040, 512), BF16), pltpu.VMEM((3, 1040, 512), BF16), pltpu.VMEM((8, 256, 768), F32)],
    )(meta, points, depth, received, inverse_y)
    edge = shifted(edge, "row", -1)
    velocity = call(
        border_kernel, shape(8, 24, 128), [SMEM, VMEM, VMEM, VMEM, VMEM], [pltpu.VMEM((24, 1152), F32)]
    )(meta, points, depth, edge, velocity)
    velocity = jnp.sum(lax.all_to_all(velocity, "col", 0, 0, tiled=True), axis=0)
    velocity = velocity.reshape(3, 1024) * live[None]
    sums = jnp.stack([jnp.sum(norm), jnp.sum(velocity * velocity)])
    sums = jnp.sum(spread_out(sums, "row"), axis=0)
    sums = jnp.sum(spread_out(sums, "col"), axis=0)
    step_length = sums[0] / sums[1]
    vorticity = spectrum * (step_length * (1.0 / math.sqrt(CELLS)))
    return vorticity, residual - step_length * velocity


def solution(mesh):
    in_specs = (
        P(None, ("row", "col")),
        P(None, ("row", "col")),
        P(("row", "col")),
        P(("row", "col")),
    )
    out_specs = (P(None, None, "col", "row", None), P(None, ("row", "col")))
    return jax.shard_map(body, mesh=mesh, in_specs=in_specs, out_specs=out_specs, check_vma=False)
```

```python
import functools
import math

import jax
import jax.numpy as jnp
import ml_dtypes
import numpy as np
from jax import lax
from jax.experimental import pallas as pl
from jax.experimental.pallas import tpu as pltpu
from jax.sharding import PartitionSpec as P

NX = 1024
NY = 1024
NZ = 64
CELLS = float(NX * NY * NZ)
TWO_PI = 2.0 * math.pi
F32 = jnp.float32
BF16 = jnp.bfloat16
VMEM_LIMIT = 56 * 1024 * 1024
VMEM = pl.BlockSpec(memory_space=pltpu.VMEM)
SMEM = pl.BlockSpec(memory_space=pltpu.SMEM)


def halves(table):
    table = table.astype(np.float32)
    high = table.astype(ml_dtypes.bfloat16)
    low = (table - high.astype(np.float32)).astype(ml_dtypes.bfloat16)
    return np.stack([high, low])


def table_y():
    first = np.arange(8)[:, None, None]
    angle = TWO_PI * ((np.arange(128)[None, :, None] * 8 + first) * np.arange(128)[None, None, :] % 1024) / 1024
    cosine, sine = np.cos(angle), np.sin(angle)
    return np.concatenate([np.concatenate([cosine, sine], 2), np.concatenate([-sine, cosine], 2)], 1)


def table_x():
    result = np.zeros((8, 2, 2, 64, 2, 64, 2))
    inner = np.arange(64)
    for first in range(8):
        for upper in range(2):
            wave = 16 * np.arange(64) + first + 8 * upper
            angle = TWO_PI * (inner[:, None] * wave[None, :] % 1024) / 1024
            result[first, upper, 0, :, 0, :, upper] = np.cos(angle)
            result[first, upper, 1, :, 0, :, upper] = np.sin(angle)
            result[first, upper, 0, :, 1, :, upper] = -np.sin(angle)
            result[first, upper, 1, :, 1, :, upper] = np.cos(angle)
    return result.reshape(8, 256, 256)


def split(value):
    high = value.astype(BF16)
    return high, (value - high.astype(F32)).astype(BF16)


def mul(left, right):
    return jnp.dot(left, right, preferred_element_type=F32)


def mul_t(left, right):
    return lax.dot_general(left, right, (((1,), (1,)), ((), ())), preferred_element_type=F32)


def small_dft(values, sign):
    count = len(values)
    if count == 1:
        return values
    even = small_dft(values[0::2], sign)
    odd = small_dft(values[1::2], sign)
    low, high = [], []
    for k in range(count // 2):
        real, imag = odd[k]
        if k > 0:
            if 4 * k == count:
                real, imag = (-imag, real) if sign > 0 else (imag, -real)
            elif 8 * k == count:
                root = math.sqrt(0.5)
                if sign > 0:
                    real, imag = (real - imag) * root, (real + imag) * root
                else:
                    real, imag = (real + imag) * root, (imag - real) * root
            elif 8 * k == 3 * count:
                root = math.sqrt(0.5)
                if sign > 0:
                    real, imag = (real + imag) * -root, (real - imag) * root
                else:
                    real, imag = (imag - real) * root, (real + imag) * -root
            else:
                cosine = math.cos(TWO_PI * k / count)
                sine = sign * math.sin(TWO_PI * k / count)
                real, imag = real * cosine - imag * sine, real * sine + imag * cosine
        low.append((even[k][0] + real, even[k][1] + imag))
        high.append((even[k][0] - real, even[k][1] - imag))
    return low + high


def hat(distance):
    return jnp.maximum(1.0 - jnp.abs(distance), 0.0)


def ramp(shape, axis):
    return lax.broadcasted_iota(jnp.int32, shape, axis).astype(F32)


def brick_place(brick):
    return brick // 64, brick // 2 % 32, brick % 2


def block_points(points, block):
    lane = pl.multiple_of(block % 8 * 128, 128)
    return points[block // 8, :, pl.ds(lane, 128)]


def depth_wave(points, meta, depth):
    index = lax.broadcasted_iota(jnp.int32, (8, 128), 0)
    mode = 4 * meta[65] + 2 * (index // 4) + index % 2
    turn = 16 * (index // 2 % 2)

    def wave(cell):
        angle = (mode * cell + turn) & 63
        value = (jnp.abs(angle - 32) - 16).astype(F32) * (math.pi / 32.0)
        square = value * value
        total = -1.0 / 39916800.0
        for factor in (1.0 / 362880.0, -1.0 / 5040.0, 1.0 / 120.0, -1.0 / 6.0, 1.0):
            total = total * square + factor
        return total * value

    def step(block, carry):
        height = block_points(points, block)[2:3]
        lower = jnp.floor(height)
        part = height - lower
        cell = lower.astype(jnp.int32) + 32 * (meta[block] % 2)
        depth[block] = (1.0 - part) * wave(cell) + part * wave(cell + 1)
        return carry

    lax.fori_loop(0, 64, step, 0, unroll=4)


def edge_weights(point):
    weight = hat(ramp((40, 128), 0) - point[1:2])
    return jnp.concatenate([weight, jnp.zeros((88, 128), F32)], 0)


def edge_waves(point, waves, place_x):
    return waves * jnp.maximum(point[0:1] - (63 - 32 * place_x).astype(F32), 0.0)


def lower_lanes(rows):
    return lax.broadcasted_iota(jnp.int32, (rows, 128), 1) < 64


def joined(first, second):
    lower = lower_lanes(first.shape[0])
    return (
        jnp.where(lower, first, pltpu.roll(second, 64, 1)),
        jnp.where(lower, pltpu.roll(first, 64, 1), second),
    )


def pack_kernel(offsets, measured, bricks, counts, out, residual):
    lane = lax.broadcasted_iota(jnp.int32, (3, 128), 1)
    for i in range(8):
        at = slice(128 * i, 128 * i + 128)
        residual[:, at] = jnp.where(lane < counts[i], measured[:, at], 0.0)
        brick = jnp.zeros((2, 128), F32) + bricks[i].astype(F32)
        block = jnp.concatenate([offsets[:, at], residual[:, at], brick], 0)
        for dest in range(8):
            out[dest, :, at] = block


def slab_weights(point, waves, place_x):
    across = hat(ramp((64, 128), 0) - (32 * place_x).astype(F32) - point[0:1])
    return jnp.concatenate([waves[i : i + 1] * across for i in range(4)], 0)


def first_spread_kernel(meta, points, table, out, depth, field, parts, windows):
    depth_wave(points, meta, depth)
    spread_kernel(0, meta, points, table, depth, out, field, parts, windows)


def spread_kernel(pair, meta, points, table, depth, out, field, parts, windows):
    field[...] = jnp.zeros_like(field)
    windows[...] = jnp.zeros_like(windows)

    def step(block, carry):
        place_x, place_y, _ = brick_place(meta[block])
        point = block_points(points, block)
        waves = depth[block][4 * pair : 4 * pair + 4]
        weight_high, weight_low = split(slab_weights(point, waves, place_x))
        along = hat(ramp((40, 128), 0) - point[1:2])
        source = jnp.concatenate([along * point[3 + c : 4 + c] for c in range(3)], 0)
        source_high, source_low = split(source)
        both = mul_t(jnp.concatenate([source_high, source_low], 0), weight_high)
        value = both[:120] + both[120:] + mul_t(source_high, weight_low)
        row = pl.multiple_of(place_y * 32, 32)
        for c in range(3):
            field[c, pl.ds(row, 40), :] += value[40 * c : 40 * c + 40]
        waves = edge_waves(point, waves, place_x)
        source_high, source_low = split(jnp.concatenate([waves[i : i + 1] * point[3:6] for i in range(4)], 0))
        weight_high, weight_low = split(edge_weights(point))
        value = mul_t(source_high, weight_high) + mul_t(source_low, weight_high) + mul_t(source_high, weight_low)
        lane = pl.multiple_of(place_y // 4 * 128, 128)
        windows[place_y % 4, :, pl.ds(lane, 128)] += value
        return carry

    lax.fori_loop(0, 64, step, 0, unroll=4)
    for c in range(3):
        field[c, 0:1, :] += field[c, 1024:1025, :]

    def outer(tile, carry):
        row = pl.multiple_of(tile * 8, 8)
        for c in range(3):
            values = [
                (field[c, pl.ds(128 * a + row, 8), 0:128], field[c, pl.ds(128 * a + row, 8), 128:256])
                for a in range(8)
            ]
            for k, (real, imag) in enumerate(small_dft(values, -1)):
                parts[k, pl.ds(row, 8), 128 * c : 128 * c + 128] = real
                parts[k, pl.ds(128 + row, 8), 128 * c : 128 * c + 128] = imag
        return carry

    lax.fori_loop(0, 16, outer, 0, unroll=2)
    total = windows[0]
    for j in range(1, 4):
        total = total + pltpu.roll(windows[j], 32 * j, 1)
    values = [(total[0:6, 128 * a : 128 * a + 128], total[6:12, 128 * a : 128 * a + 128]) for a in range(8)]
    for k, pieces in enumerate(small_dft(values, -1)):
        windows[k // 2, 0:6, 256 * (k % 2) : 256 * (k % 2) + 256] = jnp.concatenate(pieces, 1)

    def inner(k, carry):
        high, low = split(parts[k])
        value = mul(table[0, k], high) + mul(table[1, k], high) + mul(table[0, k], low)
        high, low = split(windows[k // 2, 0:6, pl.ds(pl.multiple_of(256 * (k % 2), 256), 256)])
        edge = mul_t(high, table[0, k]) + mul_t(high, table[1, k]) + mul_t(low, table[0, k])
        edge_real = joined(edge[0:3, 0:128], edge[3:6, 0:128])
        edge_imag = joined(edge[0:3, 128:256], edge[3:6, 128:256])
        for half in range(2):
            for c in range(3):
                for part in range(2):
                    row = 128 * part + 64 * half
                    to = 64 * (2 * c + part)
                    out[2 * k + half, to : to + 64] = value[row : row + 64, 128 * c : 128 * c + 128]
            out[2 * k + half, 384:392] = jnp.concatenate(
                [edge_real[half], edge_imag[half], jnp.zeros((2, 128), F32)], 0
            )
        return carry

    lax.fori_loop(0, 8, inner, 0, unroll=2)


def spectrum_kernel(pair, meta, received, table, table_back, spectrum, out, norm, parts, back, edge):
    row = meta[64]
    lane = lax.broadcasted_iota(jnp.int32, (8, 128), 1)
    edge[...] = jnp.concatenate([received[s, 384:392] for s in range(16)], 0).T

    def placed(tile, s, j):
        at = 8 * ((s + 15) % 16) + j
        first = edge[pl.ds(tile, 8), at : at + 1]
        second = edge[pl.ds(64 + tile, 8), at : at + 1]
        return received[s, pl.ds(64 * (j % 3 * 2 + j // 3) + tile, 8)] + jnp.where(
            lane == 0, first, jnp.where(lane == 64, second, 0.0)
        )

    def outer(tile, carry):
        at = pl.multiple_of(tile * 8, 8)
        for c in range(3):
            values = [(placed(at, s, c), placed(at, s, 3 + c)) for s in range(16)]
            for k, (real, imag) in enumerate(small_dft(values, -1)):
                to = 128 * (k // 8)
                first, second = joined(real, imag)
                parts[k % 8, pl.ds(128 * c + at, 8), to : to + 128] = first
                parts[k % 8, pl.ds(128 * c + 64 + at, 8), to : to + 128] = second
        return carry

    lax.fori_loop(0, 8, outer, 0)

    index_y = 8 * (64 * (row % 2) + lax.broadcasted_iota(jnp.int32, (64, 128), 0)) + row // 2
    lane_x = lax.broadcasted_iota(jnp.int32, (64, 128), 1)
    wave_y = jnp.where(index_y < NY // 2, index_y, index_y - NY).astype(F32) * (TWO_PI / NY)

    def inner(k, total):
        high, low = split(parts[k])
        value = mul(high, table[0, k]) + mul(low, table[0, k]) + mul(high, table[1, k])
        index_x = 8 * lane_x + k
        wave_x = jnp.where(index_x < NX // 2, index_x, index_x - NX).astype(F32) * (TWO_PI / NX)
        flat = wave_x * wave_x + wave_y * wave_y
        valid = (index_y != NY // 2) & (index_x != NX // 2)
        to = pl.multiple_of(k * 128, 128)
        rows = [[None, None] for _ in range(3)]
        for h in range(2):
            index_z = 4 * meta[65] + 2 * pair + h
            wave_z = index_z.astype(F32) * (TWO_PI / NZ)
            weight = jnp.where(index_z == 0, 1.0, 2.0).astype(F32) / CELLS
            squared = flat + wave_z * wave_z
            keep = valid & (squared > 0.0)
            inverse = jnp.where(keep, 1.0 / jnp.where(keep, squared, 1.0), 0.0)

            def crossed(vector, scale):
                return [
                    (wave_y * vector[2] - wave_z * vector[1]) * scale,
                    (wave_z * vector[0] - wave_x * vector[2]) * scale,
                    (wave_x * vector[1] - wave_y * vector[0]) * scale,
                ]

            start = [128 * c + 64 * h for c in range(3)]
            real = [value[s : s + 64, 0:128] for s in start]
            imag = [value[s : s + 64, 128:256] for s in start]
            grad_real = crossed(imag, -inverse)
            grad_imag = crossed(real, inverse)
            square = 0.0
            for c in range(3):
                spectrum[0, c, h, :, pl.ds(to, 128)] = grad_real[c]
                spectrum[1, c, h, :, pl.ds(to, 128)] = grad_imag[c]
                square = square + grad_real[c] * grad_real[c] + grad_imag[c] * grad_imag[c]
            total = total + weight * square
            scale = inverse * weight
            back_real = crossed(grad_imag, -scale)
            back_imag = crossed(grad_real, scale)
            for c in range(3):
                rows[c][h] = jnp.concatenate([back_real[c], back_imag[c]], 1)
        high, low = split(jnp.concatenate([rows[c][h] for c in range(3) for h in range(2)], 0))
        back[k] = mul(high, table_back[0, k]) + mul(low, table_back[0, k]) + mul(high, table_back[1, k])
        return total

    total = lax.fori_loop(0, 8, inner, jnp.zeros((64, 128), F32))
    norm[...] = jnp.sum(total.reshape(8, 8, 128), axis=0)

    def last(tile, carry):
        at = pl.multiple_of(tile * 8, 8)
        columns = [jnp.zeros((8, 128), F32), jnp.zeros((8, 128), F32)]
        for c in range(3):
            values = []
            for k in range(16):
                to = 128 * (k // 8)
                first = back[k % 8, pl.ds(128 * c + at, 8), to : to + 128]
                second = back[k % 8, pl.ds(128 * c + 64 + at, 8), to : to + 128]
                values.append(joined(first, second))
            for s, pieces in enumerate(small_dft(values, 1)):
                for part in range(2):
                    piece = pieces[part]
                    out[s, pl.ds(64 * (2 * c + part) + at, 8)] = piece
                    place = lane == 8 * ((s + 15) % 16) + 3 * part + c
                    for h in range(2):
                        columns[h] = jnp.where(place, piece[:, 64 * h : 64 * h + 1], columns[h])
        for h in range(2):
            edge[pl.ds(64 * h + at, 8), :] = columns[h]
        return carry

    lax.fori_loop(0, 8, last, 0)
    turned = edge[...].T
    for s in range(16):
        out[s, 384:392] = turned[8 * s : 8 * s + 8]


def gather_kernel(pair, meta, points, depth, received, table, out, field_high, field_low, parts, edge, windows):
    def inner(k, carry):
        columns = [
            jnp.concatenate(
                [
                    received[2 * k + half, 64 * (2 * c + part) : 64 * (2 * c + part) + 64]
                    for part in range(2)
                    for half in range(2)
                ],
                0,
            )
            for c in range(3)
        ]
        high, low = split(jnp.concatenate(columns, 1))
        parts[k] = mul(table[0, k], high) + mul(table[1, k], high) + mul(table[0, k], low)
        first, second = joined(received[2 * k, 384:392], received[2 * k + 1, 384:392])
        real = jnp.concatenate([first[0:3], second[0:3]], 0)
        imag = jnp.concatenate([first[3:6], second[3:6]], 0)
        high, low = split(jnp.concatenate([real, imag], 1))
        edge[k] = mul_t(high, table[0, k]) + mul_t(high, table[1, k]) + mul_t(low, table[0, k])
        return carry

    lax.fori_loop(0, 8, inner, 0, unroll=2)
    values = [(edge[k, :, 0:128], edge[k, :, 128:256]) for k in range(8)]
    plane = jnp.concatenate([jnp.concatenate(pieces, 0) for pieces in small_dft(values, 1)], 1)
    for j in range(4):
        windows[j] = plane if j == 0 else pltpu.roll(plane, 1024 - 32 * j, 1)

    def outer(tile, carry):
        row = pl.multiple_of(tile * 16, 16)
        for c in range(3):
            at = 128 * c
            values = [
                (parts[k, pl.ds(row, 16), at : at + 128], parts[k, pl.ds(128 + row, 16), at : at + 128])
                for k in range(8)
            ]
            for a, pieces in enumerate(small_dft(values, 1)):
                for part in range(2):
                    high, low = split(pieces[part])
                    lane = 128 * part
                    field_high[c, pl.ds(128 * a + row, 16), lane : lane + 128] = high
                    field_low[c, pl.ds(128 * a + row, 16), lane : lane + 128] = low
        return carry

    lax.fori_loop(0, 8, outer, 0)
    for c in range(3):
        field_high[c, 1024:1040, :] = field_high[c, 0:16, :]
        field_low[c, 1024:1040, :] = field_low[c, 0:16, :]

    def step(block, carry):
        place_x, place_y, _ = brick_place(meta[block])
        point = block_points(points, block)
        waves = depth[block][4 * pair : 4 * pair + 4]
        weight_high, weight_low = split(slab_weights(point, waves, place_x))
        weights = jnp.concatenate([weight_high, weight_low], 1)
        along = hat(ramp((48, 128), 0) - point[1:2])
        row = pl.multiple_of(place_y * 32, 32)
        high = jnp.concatenate([field_high[c, pl.ds(row, 48), :] for c in range(3)], 0)
        low = jnp.concatenate([field_low[c, pl.ds(row, 48), :] for c in range(3)], 0)
        both = mul(high, weights)
        value = both[:, :128] + both[:, 128:] + mul(low, weight_high)
        velocity = [jnp.sum(along * value[48 * c : 48 * c + 48], axis=0, keepdims=True) for c in range(3)]
        waves = edge_waves(point, waves, place_x)
        weight_high, weight_low = split(edge_weights(point))
        lane = pl.multiple_of(place_y // 4 * 128, 128)
        high, low = split(windows[place_y % 4, :, pl.ds(lane, 128)])
        value = mul(high, weight_high) + mul(low, weight_high) + mul(high, weight_low)
        more = sum(waves[i : i + 1] * value[3 * i : 3 * i + 3] for i in range(4))
        for c in range(3):
            out[block // 8, pl.ds(8 * c + block % 8, 1), :] = velocity[c] + more[c : c + 1]
        return carry

    lax.fori_loop(0, 64, step, 0, unroll=4)


def sums_kernel(counts, received, first_norm, second_norm, velocity, out):
    row = lax.broadcasted_iota(jnp.int32, (8, 128), 0)
    count = jnp.zeros((8, 128), jnp.int32)
    for i in range(8):
        count = jnp.where(row == i, counts[i], count)
    live = lax.broadcasted_iota(jnp.int32, (8, 128), 1) < count
    square = jnp.zeros((8, 128), F32)
    for c in range(3):
        total = received[0, 8 * c : 8 * c + 8]
        for source in range(1, 8):
            total = total + received[source, 8 * c : 8 * c + 8]
        total = jnp.where(live, total, 0.0)
        square = square + total * total
        for i in range(8):
            velocity[c : c + 1, 128 * i : 128 * i + 128] = total[i : i + 1]
    norm = jnp.sum(first_norm[...] + second_norm[...], axis=0, keepdims=True)
    square = jnp.sum(square, axis=0, keepdims=True)
    tile = jnp.where(row == 0, norm, jnp.where(row == 1, square, 0.0))
    for dest in range(16):
        out[dest] = tile


def final_kernel(sums, residual, velocity, first, second, spectrum, out):
    total = jnp.sum(jnp.sum(sums[...], axis=0), axis=1, keepdims=True)
    length = total[0:1] / total[1:2]
    part, c = pl.program_id(0), pl.program_id(1)
    scale = length * (1.0 / math.sqrt(CELLS))
    spectrum[0, 0, 0:2] = first[part, c] * scale
    spectrum[0, 0, 2:4] = second[part, c] * scale
    out[...] = residual[...] - length * velocity[...]


def call(kernel, outs, specs, scratch=(), traffic=0):
    return pl.pallas_call(
        kernel,
        out_shape=outs,
        in_specs=specs,
        scratch_shapes=list(scratch),
        cost_estimate=pl.CostEstimate(flops=0, bytes_accessed=int(traffic), transcendentals=0),
        compiler_params=pltpu.CompilerParams(vmem_limit_bytes=VMEM_LIMIT),
    )


def shape(*dims):
    return jax.ShapeDtypeStruct(dims, F32)


def spread_out(value, axis):
    count = lax.axis_size(axis)
    return lax.all_to_all(jnp.broadcast_to(value[None], (count,) + value.shape), axis, 0, 0, tiled=True)


def exchange(value):
    return lax.all_to_all(value, "row", 0, 0, tiled=True)


def body(offsets, measured, block_brick, block_count):
    row = lax.axis_index("row")
    col = lax.axis_index("col")
    packed, residual = call(
        pack_kernel, (shape(8, 8, 1024), shape(3, 1024)), [VMEM, VMEM, SMEM, SMEM], traffic=1e6
    )(offsets, measured, block_brick, block_count)
    points = lax.all_to_all(packed, "col", 0, 0, tiled=True)
    bricks = points[:, 6, ::128].reshape(64).astype(jnp.int32)
    meta = jnp.concatenate([bricks, jnp.stack([row, col]).astype(jnp.int32)])
    y_table = table_y()
    x_table = table_x()
    forward_y = jnp.asarray(halves(y_table))
    inverse_y = jnp.asarray(halves(y_table.transpose(0, 2, 1)))
    forward_x = jnp.asarray(halves(x_table))
    inverse_x = jnp.asarray(halves(x_table.transpose(0, 2, 1)))

    scratch = [pltpu.VMEM((3, 1032, 256), F32), pltpu.VMEM((8, 256, 384), F32), pltpu.VMEM((4, 12, 1024), F32)]
    sent, depth = call(
        first_spread_kernel, (shape(16, 392, 128), shape(64, 8, 128)), [SMEM, VMEM, VMEM], scratch, 40e6
    )(meta, points, forward_y)
    received = [exchange(sent)]
    sent = call(
        functools.partial(spread_kernel, 1), shape(16, 392, 128), [SMEM, VMEM, VMEM, VMEM], scratch, 40e6
    )(meta, points, forward_y, depth)
    received.append(exchange(sent))
    spectra = []
    norms = []
    for pair in range(2):
        spectrum, sent, norm = call(
            functools.partial(spectrum_kernel, pair),
            (shape(2, 3, 2, 64, 1024), shape(16, 392, 128), shape(8, 128)),
            [SMEM, VMEM, VMEM, VMEM],
            [pltpu.VMEM((8, 384, 256), F32), pltpu.VMEM((8, 384, 256), F32), pltpu.VMEM((128, 128), F32)],
            40e6,
        )(meta, received[pair], forward_x, inverse_x)
        spectra.append(spectrum)
        norms.append(norm)
        received[pair] = exchange(sent)
    velocities = [
        call(
            functools.partial(gather_kernel, pair),
            shape(8, 24, 128),
            [SMEM, VMEM, VMEM, VMEM, VMEM],
            [
                pltpu.VMEM((3, 1040, 256), BF16),
                pltpu.VMEM((3, 1040, 256), BF16),
                pltpu.VMEM((8, 256, 384), F32),
                pltpu.VMEM((8, 6, 256), F32),
                pltpu.VMEM((4, 12, 1024), F32),
            ],
            40e6,
        )(meta, points, depth, received[pair], inverse_y)
        for pair in range(2)
    ]
    velocity = lax.all_to_all(velocities[0] + velocities[1], "col", 0, 0, tiled=True)
    velocity, sums = call(sums_kernel, (shape(3, 1024), shape(16, 8, 128)), [SMEM] + [VMEM] * 3, traffic=1e6)(
        block_count, velocity, *norms
    )
    sums = lax.all_to_all(sums, "row", 0, 0, tiled=True)
    sums = spread_out(jnp.sum(sums, axis=0), "col")
    return pl.pallas_call(
        final_kernel,
        grid=(2, 3),
        out_shape=(shape(2, 3, 4, 64, 1024), shape(3, 1024)),
        in_specs=[VMEM] * 5,
        out_specs=(pl.BlockSpec((1, 1, 4, 64, 1024), lambda i, j: (i, j, 0, 0, 0)), VMEM),
        cost_estimate=pl.CostEstimate(flops=0, bytes_accessed=13_000_000, transcendentals=0),
        compiler_params=pltpu.CompilerParams(vmem_limit_bytes=VMEM_LIMIT),
    )(sums, residual, velocity, *spectra)


def solution(mesh):
    in_specs = (
        P(None, ("row", "col")),
        P(None, ("row", "col")),
        P(("row", "col")),
        P(("row", "col")),
    )
    out_specs = (P(None, None, "col", "row", None), P(None, ("row", "col")))
    return jax.shard_map(body, mesh=mesh, in_specs=in_specs, out_specs=out_specs, check_vma=False)
```

```python
import functools
import math

import jax
import jax.numpy as jnp
import ml_dtypes
import numpy as np
from jax import lax
from jax.experimental import pallas as pl
from jax.experimental.pallas import tpu as pltpu
from jax.sharding import PartitionSpec as P

NX = 1024
NY = 1024
NZ = 64
CELLS = float(NX * NY * NZ)
TWO_PI = 2.0 * math.pi
F32 = jnp.float32
BF16 = jnp.bfloat16
VMEM_LIMIT = 64 * 1024 * 1024
VMEM = pl.BlockSpec(memory_space=pltpu.VMEM)
SMEM = pl.BlockSpec(memory_space=pltpu.SMEM)
ANY = pl.BlockSpec(memory_space=pl.ANY)
TABLE = pltpu.VMEM((8, 2, 256, 256), BF16)
BLOCKS = pltpu.VMEM((16, 392, 128), F32)


def halves(table):
    table = table.astype(np.float32)
    high = table.astype(ml_dtypes.bfloat16)
    low = (table - high.astype(np.float32)).astype(ml_dtypes.bfloat16)
    return np.stack([high, low], 1)


def table_y():
    first = np.arange(8)[:, None, None]
    angle = TWO_PI * ((np.arange(128)[None, :, None] * 8 + first) * np.arange(128)[None, None, :] % 1024) / 1024
    cosine, sine = np.cos(angle), np.sin(angle)
    return np.concatenate([np.concatenate([cosine, sine], 2), np.concatenate([-sine, cosine], 2)], 1)


def table_x():
    result = np.zeros((8, 2, 2, 64, 2, 64, 2))
    inner = np.arange(64)
    for first in range(8):
        for upper in range(2):
            wave = 16 * np.arange(64) + first + 8 * upper
            angle = TWO_PI * (inner[:, None] * wave[None, :] % 1024) / 1024
            result[first, upper, 0, :, 0, :, upper] = np.cos(angle)
            result[first, upper, 1, :, 0, :, upper] = np.sin(angle)
            result[first, upper, 0, :, 1, :, upper] = -np.sin(angle)
            result[first, upper, 1, :, 1, :, upper] = np.cos(angle)
    return result.reshape(8, 256, 256)


def split(value):
    high = value.astype(BF16)
    return high, (value - high.astype(F32)).astype(BF16)


def mul(left, right):
    return jnp.dot(left, right, preferred_element_type=F32)


def mul_t(left, right):
    return lax.dot_general(left, right, (((1,), (1,)), ((), ())), preferred_element_type=F32)


def doubled(high, low):
    return jnp.concatenate(
        [jnp.concatenate([high, high], 1), jnp.concatenate([low, jnp.zeros_like(low)], 1)], 0
    )


def small_dft(values, sign):
    count = len(values)
    if count == 1:
        return values
    even = small_dft(values[0::2], sign)
    odd = small_dft(values[1::2], sign)
    low, high = [], []
    for k in range(count // 2):
        real, imag = odd[k]
        if k > 0:
            if 4 * k == count:
                real, imag = (-imag, real) if sign > 0 else (imag, -real)
            elif 8 * k == count:
                root = math.sqrt(0.5)
                if sign > 0:
                    real, imag = (real - imag) * root, (real + imag) * root
                else:
                    real, imag = (real + imag) * root, (imag - real) * root
            elif 8 * k == 3 * count:
                root = math.sqrt(0.5)
                if sign > 0:
                    real, imag = (real + imag) * -root, (real - imag) * root
                else:
                    real, imag = (imag - real) * root, (real + imag) * -root
            else:
                cosine = math.cos(TWO_PI * k / count)
                sine = sign * math.sin(TWO_PI * k / count)
                real, imag = real * cosine - imag * sine, real * sine + imag * cosine
        low.append((even[k][0] + real, even[k][1] + imag))
        high.append((even[k][0] - real, even[k][1] - imag))
    return low + high


def hat(distance):
    return jnp.maximum(1.0 - jnp.abs(distance), 0.0)


def ramp(shape, axis):
    return lax.broadcasted_iota(jnp.int32, shape, axis).astype(F32)


def brick_place(brick):
    return brick // 64, brick // 2 % 32, brick % 2


def block_points(points, block):
    lane = pl.multiple_of(block % 8 * 128, 128)
    return points[block // 8, :, pl.ds(lane, 128)]


def depth_wave(points, meta, depth):
    index = lax.broadcasted_iota(jnp.int32, (8, 128), 0)
    mode = 4 * meta[65] + 2 * (index // 4) + index % 2
    turn = 16 * (index // 2 % 2)

    def wave(cell):
        angle = (mode * cell + turn) & 63
        value = (jnp.abs(angle - 32) - 16).astype(F32) * (math.pi / 32.0)
        square = value * value
        total = -1.0 / 39916800.0
        for factor in (1.0 / 362880.0, -1.0 / 5040.0, 1.0 / 120.0, -1.0 / 6.0, 1.0):
            total = total * square + factor
        return total * value

    def step(block, carry):
        height = block_points(points, block)[2:3]
        lower = jnp.floor(height)
        part = height - lower
        cell = lower.astype(jnp.int32) + 32 * (meta[block] % 2)
        depth[block] = (1.0 - part) * wave(cell) + part * wave(cell + 1)
        return carry

    lax.fori_loop(0, 64, step, 0, unroll=32)


def edge_weights(along):
    return jnp.concatenate([along[:40], jnp.zeros((88, 128), F32)], 0)


def edge_waves(point, waves, place_x):
    return waves * jnp.maximum(point[0:1] - (63 - 32 * place_x).astype(F32), 0.0)


def lower_lanes(rows):
    return lax.broadcasted_iota(jnp.int32, (rows, 128), 1) < 64


def joined(first, second):
    lower = lower_lanes(first.shape[0])
    return (
        jnp.where(lower, first, pltpu.roll(second, 64, 1)),
        jnp.where(lower, pltpu.roll(first, 64, 1), second),
    )


def pack_kernel(offsets, measured, bricks, counts, out, residual):
    lane = lax.broadcasted_iota(jnp.int32, (3, 128), 1)
    for i in range(8):
        at = slice(128 * i, 128 * i + 128)
        residual[:, at] = jnp.where(lane < counts[i], measured[:, at], 0.0)
        brick = jnp.zeros((2, 128), F32) + bricks[i].astype(F32)
        block = jnp.concatenate([offsets[:, at], residual[:, at], brick], 0)
        for dest in range(8):
            out[dest, :, at] = block


def slab_weights(point, waves, place_x):
    across = hat(ramp((64, 128), 0) - (32 * place_x).astype(F32) - point[0:1])
    return jnp.concatenate([waves[i : i + 1] * across for i in range(4)], 0)


def first_spread_kernel(meta, points, table, out, depth, *scratch):
    depth_wave(points, meta, depth)
    spread_kernel(0, meta, points, table, depth, out, *scratch)


def spread_kernel(
    pair, meta, points, far_table, depth, far_out, field, parts, windows, table, out, table_done, out_done
):
    def table_copy(k):
        return pltpu.make_async_copy(far_table.at[k], table.at[k], table_done.at[k])

    def out_copy(k):
        at = pl.ds(2 * k, 2)
        return pltpu.make_async_copy(out.at[at], far_out.at[at], out_done.at[k])

    for k in range(8):
        table_copy(k).start()
    field[...] = jnp.zeros_like(field)
    windows[...] = jnp.zeros_like(windows)

    def step(block, carry):
        place_x, place_y, _ = brick_place(meta[block])
        point = block_points(points, block)
        waves = depth[block][4 * pair : 4 * pair + 4]
        weight_high, weight_low = split(slab_weights(point, waves, place_x))
        along = hat(ramp((40, 128), 0) - point[1:2])
        source = jnp.concatenate([along * point[3 + c : 4 + c] for c in range(3)], 0)
        source_high, source_low = split(source)
        both = mul_t(doubled(source_high, source_low), jnp.concatenate([weight_high, weight_low], 1))
        value = both[:120] + both[120:]
        row = pl.multiple_of(place_y * 32, 32)
        for c in range(3):
            field[c, pl.ds(row, 40), :] += value[40 * c : 40 * c + 40]
        waves = edge_waves(point, waves, place_x)
        source_high, source_low = split(jnp.concatenate([waves[i : i + 1] * point[3:6] for i in range(4)], 0))
        weight_high, weight_low = split(edge_weights(along))
        both = mul_t(doubled(source_high, source_low), jnp.concatenate([weight_high, weight_low], 1))
        value = both[:12] + both[12:]
        lane = pl.multiple_of(place_y // 4 * 128, 128)
        windows[place_y % 4, :, pl.ds(lane, 128)] += value
        return carry

    lax.fori_loop(0, 64, step, 0, unroll=32)
    for c in range(3):
        field[c, 0:1, :] += field[c, 1024:1025, :]

    def outer(tile, carry):
        row = pl.multiple_of(tile * 8, 8)
        for c in range(3):
            values = [
                (field[c, pl.ds(128 * a + row, 8), 0:128], field[c, pl.ds(128 * a + row, 8), 128:256])
                for a in range(8)
            ]
            for k, (real, imag) in enumerate(small_dft(values, -1)):
                parts[k, pl.ds(row, 8), 128 * c : 128 * c + 128] = real
                parts[k, pl.ds(128 + row, 8), 128 * c : 128 * c + 128] = imag
        return carry

    lax.fori_loop(0, 16, outer, 0, unroll=2)
    total = windows[0]
    for j in range(1, 4):
        total = total + pltpu.roll(windows[j], 32 * j, 1)
    values = [(total[0:6, 128 * a : 128 * a + 128], total[6:12, 128 * a : 128 * a + 128]) for a in range(8)]
    for k, pieces in enumerate(small_dft(values, -1)):
        windows[k // 2, 0:6, 256 * (k % 2) : 256 * (k % 2) + 256] = jnp.concatenate(pieces, 1)

    def inner(k, carry):
        table_copy(k).wait()
        high, low = split(parts[k])
        value = mul(table[k, 0], high) + mul(table[k, 1], high) + mul(table[k, 0], low)
        high, low = split(windows[k // 2, 0:6, pl.ds(pl.multiple_of(256 * (k % 2), 256), 256)])
        edge = mul_t(high, table[k, 0]) + mul_t(high, table[k, 1]) + mul_t(low, table[k, 0])
        edge_real = joined(edge[0:3, 0:128], edge[3:6, 0:128])
        edge_imag = joined(edge[0:3, 128:256], edge[3:6, 128:256])
        for half in range(2):
            for c in range(3):
                for part in range(2):
                    row = 128 * part + 64 * half
                    to = 64 * (2 * c + part)
                    out[2 * k + half, to : to + 64] = value[row : row + 64, 128 * c : 128 * c + 128]
            out[2 * k + half, 384:392] = jnp.concatenate(
                [edge_real[half], edge_imag[half], jnp.zeros((2, 128), F32)], 0
            )
        out_copy(k).start()
        return carry

    lax.fori_loop(0, 8, inner, 0)
    for k in range(8):
        out_copy(k).wait()


def spectrum_kernel(
    pair, meta, far_received, table, table_back, spectrum, out, norm, parts, back, edge, received, done
):
    def copy(c):
        at = pl.ds(128 * c, 128 if c < 3 else 8)
        return pltpu.make_async_copy(far_received.at[:, at], received.at[:, at], done.at[c])

    for c in (3, 0, 1, 2):
        copy(c).start()
    copy(3).wait()
    row = meta[64]
    lane = lax.broadcasted_iota(jnp.int32, (8, 128), 1)
    edge[...] = jnp.concatenate([received[s, 384:392] for s in range(16)], 0).T

    def placed(tile, s, j):
        at = 8 * ((s + 15) % 16) + j
        first = edge[pl.ds(tile, 8), at : at + 1]
        second = edge[pl.ds(64 + tile, 8), at : at + 1]
        return received[s, pl.ds(64 * (j % 3 * 2 + j // 3) + tile, 8)] + jnp.where(
            lane == 0, first, jnp.where(lane == 64, second, 0.0)
        )

    def outer(c, tile, carry):
        at = pl.multiple_of(tile * 8, 8)
        values = [(placed(at, s, c), placed(at, s, 3 + c)) for s in range(16)]
        for k, (real, imag) in enumerate(small_dft(values, -1)):
            to = 128 * (k // 8)
            first, second = joined(real, imag)
            parts[k % 8, pl.ds(128 * c + at, 8), to : to + 128] = first
            parts[k % 8, pl.ds(128 * c + 64 + at, 8), to : to + 128] = second
        return carry

    for c in range(3):
        copy(c).wait()
        lax.fori_loop(0, 8, functools.partial(outer, c), 0)

    index_y = 8 * (64 * (row % 2) + lax.broadcasted_iota(jnp.int32, (64, 128), 0)) + row // 2
    lane_x = lax.broadcasted_iota(jnp.int32, (64, 128), 1)
    wave_y = jnp.where(index_y < NY // 2, index_y, index_y - NY).astype(F32) * (TWO_PI / NY)

    def inner(k, total):
        high, low = split(parts[k])
        value = mul(high, table[k, 0]) + mul(low, table[k, 0]) + mul(high, table[k, 1])
        index_x = 8 * lane_x + k
        wave_x = jnp.where(index_x < NX // 2, index_x, index_x - NX).astype(F32) * (TWO_PI / NX)
        flat = wave_x * wave_x + wave_y * wave_y
        valid = (index_y != NY // 2) & (index_x != NX // 2)
        to = pl.multiple_of(k * 128, 128)
        rows = [[None, None] for _ in range(3)]
        for h in range(2):
            index_z = 4 * meta[65] + 2 * pair + h
            wave_z = index_z.astype(F32) * (TWO_PI / NZ)
            weight = jnp.where(index_z == 0, 1.0, 2.0).astype(F32) / CELLS
            squared = flat + wave_z * wave_z
            keep = valid & (squared > 0.0)
            inverse = jnp.where(keep, 1.0 / jnp.where(keep, squared, 1.0), 0.0)

            def crossed(vector, scale):
                return [
                    (wave_y * vector[2] - wave_z * vector[1]) * scale,
                    (wave_z * vector[0] - wave_x * vector[2]) * scale,
                    (wave_x * vector[1] - wave_y * vector[0]) * scale,
                ]

            start = [128 * c + 64 * h for c in range(3)]
            real = [value[s : s + 64, 0:128] for s in start]
            imag = [value[s : s + 64, 128:256] for s in start]
            grad_real = crossed(imag, -inverse)
            grad_imag = crossed(real, inverse)
            square = 0.0
            for c in range(3):
                spectrum[0, c, h, :, pl.ds(to, 128)] = grad_real[c]
                spectrum[1, c, h, :, pl.ds(to, 128)] = grad_imag[c]
                square = square + grad_real[c] * grad_real[c] + grad_imag[c] * grad_imag[c]
            total = total + weight * square
            scale = inverse * weight
            back_real = crossed(grad_imag, -scale)
            back_imag = crossed(grad_real, scale)
            for c in range(3):
                rows[c][h] = jnp.concatenate([back_real[c], back_imag[c]], 1)
        high, low = split(jnp.concatenate([rows[c][h] for c in range(3) for h in range(2)], 0))
        back[k] = mul(high, table_back[k, 0]) + mul(low, table_back[k, 0]) + mul(high, table_back[k, 1])
        return total

    total = lax.fori_loop(0, 8, inner, jnp.zeros((64, 128), F32))
    norm[...] = jnp.sum(total.reshape(8, 8, 128), axis=0)

    def last(tile, carry):
        at = pl.multiple_of(tile * 8, 8)
        columns = [jnp.zeros((8, 128), F32), jnp.zeros((8, 128), F32)]
        for c in range(3):
            values = []
            for k in range(16):
                to = 128 * (k // 8)
                first = back[k % 8, pl.ds(128 * c + at, 8), to : to + 128]
                second = back[k % 8, pl.ds(128 * c + 64 + at, 8), to : to + 128]
                values.append(joined(first, second))
            for s, pieces in enumerate(small_dft(values, 1)):
                for part in range(2):
                    piece = pieces[part]
                    out[s, pl.ds(64 * (2 * c + part) + at, 8)] = piece
                    place = lane == 8 * ((s + 15) % 16) + 3 * part + c
                    for h in range(2):
                        columns[h] = jnp.where(place, piece[:, 64 * h : 64 * h + 1], columns[h])
        for h in range(2):
            edge[pl.ds(64 * h + at, 8), :] = columns[h]
        return carry

    lax.fori_loop(0, 8, last, 0)
    turned = edge[...].T
    for s in range(16):
        out[s, 384:392] = turned[8 * s : 8 * s + 8]


def first_gather_kernel(meta, points, depth, received, table, out, *scratch):
    gather_kernel(0, meta, points, depth, None, received, table, out, *scratch)


def gather_kernel(
    pair, meta, points, depth, earlier, far_received, far_table, out,
    field_high, field_low, parts, edge, windows, table, received, table_done, received_done,
):
    def table_copy(k):
        return pltpu.make_async_copy(far_table.at[k], table.at[k], table_done.at[k])

    def received_copy(k):
        at = pl.ds(2 * k, 2)
        return pltpu.make_async_copy(far_received.at[at], received.at[at], received_done.at[k])

    for k in range(8):
        table_copy(k).start()
        received_copy(k).start()

    def inner(k, carry):
        table_copy(k).wait()
        received_copy(k).wait()
        columns = [
            jnp.concatenate(
                [
                    received[2 * k + half, 64 * (2 * c + part) : 64 * (2 * c + part) + 64]
                    for part in range(2)
                    for half in range(2)
                ],
                0,
            )
            for c in range(3)
        ]
        high, low = split(jnp.concatenate(columns, 1))
        parts[k] = mul(table[k, 0], high) + mul(table[k, 1], high) + mul(table[k, 0], low)
        first, second = joined(received[2 * k, 384:392], received[2 * k + 1, 384:392])
        real = jnp.concatenate([first[0:3], second[0:3]], 0)
        imag = jnp.concatenate([first[3:6], second[3:6]], 0)
        high, low = split(jnp.concatenate([real, imag], 1))
        edge[k] = mul_t(high, table[k, 0]) + mul_t(high, table[k, 1]) + mul_t(low, table[k, 0])
        return carry

    lax.fori_loop(0, 8, inner, 0)
    values = [(edge[k, :, 0:128], edge[k, :, 128:256]) for k in range(8)]
    plane = jnp.concatenate([jnp.concatenate(pieces, 0) for pieces in small_dft(values, 1)], 1)
    for j in range(4):
        windows[j] = plane if j == 0 else pltpu.roll(plane, 1024 - 32 * j, 1)

    def outer(tile, carry):
        row = pl.multiple_of(tile * 16, 16)
        for c in range(3):
            at = 128 * c
            values = [
                (parts[k, pl.ds(row, 16), at : at + 128], parts[k, pl.ds(128 + row, 16), at : at + 128])
                for k in range(8)
            ]
            for a, pieces in enumerate(small_dft(values, 1)):
                for part in range(2):
                    high, low = split(pieces[part])
                    lane = 128 * part
                    field_high[c, pl.ds(128 * a + row, 16), lane : lane + 128] = high
                    field_low[c, pl.ds(128 * a + row, 16), lane : lane + 128] = low
        return carry

    lax.fori_loop(0, 8, outer, 0)
    for c in range(3):
        field_high[c, 1024:1040, :] = field_high[c, 0:16, :]
        field_low[c, 1024:1040, :] = field_low[c, 0:16, :]

    def step(block, carry):
        place_x, place_y, _ = brick_place(meta[block])
        point = block_points(points, block)
        waves = depth[block][4 * pair : 4 * pair + 4]
        weight_high, weight_low = split(slab_weights(point, waves, place_x))
        weights = jnp.concatenate([weight_high, weight_low], 1)
        along = hat(ramp((48, 128), 0) - point[1:2])
        row = pl.multiple_of(place_y * 32, 32)
        high = jnp.concatenate([field_high[c, pl.ds(row, 48), :] for c in range(3)], 0)
        low = jnp.concatenate([field_low[c, pl.ds(row, 48), :] for c in range(3)], 0)
        both = mul(high, weights)
        value = both[:, :128] + both[:, 128:] + mul(low, weight_high)
        velocity = [jnp.sum(along * value[48 * c : 48 * c + 48], axis=0, keepdims=True) for c in range(3)]
        waves = edge_waves(point, waves, place_x)
        weight_high, weight_low = split(edge_weights(along))
        lane = pl.multiple_of(place_y // 4 * 128, 128)
        high, low = split(windows[place_y % 4, :, pl.ds(lane, 128)])
        value = mul(high, weight_high) + mul(low, weight_high) + mul(high, weight_low)
        more = sum(waves[i : i + 1] * value[3 * i : 3 * i + 3] for i in range(4))
        for c in range(3):
            at = pl.ds(8 * c + block % 8, 1)
            total = velocity[c] + more[c : c + 1]
            if earlier is not None:
                total = total + earlier[block // 8, at, :]
            out[block // 8, at, :] = total
        return carry

    lax.fori_loop(0, 64, step, 0, unroll=32)


def sums_kernel(counts, received, first_norm, second_norm, velocity, out):
    row = lax.broadcasted_iota(jnp.int32, (8, 128), 0)
    count = jnp.zeros((8, 128), jnp.int32)
    for i in range(8):
        count = jnp.where(row == i, counts[i], count)
    live = lax.broadcasted_iota(jnp.int32, (8, 128), 1) < count
    square = jnp.zeros((8, 128), F32)
    for c in range(3):
        total = received[0, 8 * c : 8 * c + 8]
        for source in range(1, 8):
            total = total + received[source, 8 * c : 8 * c + 8]
        total = jnp.where(live, total, 0.0)
        square = square + total * total
        for i in range(8):
            velocity[c : c + 1, 128 * i : 128 * i + 128] = total[i : i + 1]
    norm = jnp.sum(first_norm[...] + second_norm[...], axis=0, keepdims=True)
    square = jnp.sum(square, axis=0, keepdims=True)
    tile = jnp.where(row == 0, norm, jnp.where(row == 1, square, 0.0))
    for dest in range(16):
        out[dest] = tile


def final_kernel(sums, residual, velocity, first, second, spectrum, out, values, loaded, stored):
    def load(i):
        source = (first, second)[i % 2]
        return pltpu.make_async_copy(source.at[i // 6, i // 2 % 3], values.at[i], loaded.at[i])

    def store(i):
        place = spectrum.at[i // 6, i // 2 % 3, pl.ds(i % 2 * 2, 2)]
        return pltpu.make_async_copy(values.at[i], place, stored.at[i])

    for i in range(12):
        load(i).start()
    total = jnp.sum(jnp.sum(sums[...], axis=0), axis=1, keepdims=True)
    length = total[0:1] / total[1:2]
    scale = length * (1.0 / math.sqrt(CELLS))
    for i in range(12):
        load(i).wait()
        values[i] = values[i] * scale
        store(i).start()
    out[...] = residual[...] - length * velocity[...]
    for i in range(12):
        store(i).wait()


def filled(kernel):
    return lambda *refs: kernel(*refs[:-1])


def call(kernel, outs, specs, scratch=(), traffic=0, out_specs=VMEM, fill=1):
    return pl.pallas_call(
        filled(kernel),
        out_shape=outs,
        in_specs=specs,
        out_specs=out_specs,
        scratch_shapes=list(scratch) + [pltpu.VMEM((fill * 2048, 128), F32)],
        cost_estimate=pl.CostEstimate(flops=0, bytes_accessed=int(traffic), transcendentals=0),
        compiler_params=pltpu.CompilerParams(vmem_limit_bytes=VMEM_LIMIT),
    )


def shape(*dims):
    return jax.ShapeDtypeStruct(dims, F32)


def spread_out(value, axis):
    count = lax.axis_size(axis)
    return lax.all_to_all(jnp.broadcast_to(value[None], (count,) + value.shape), axis, 0, 0, tiled=True)


def exchange(value):
    return lax.all_to_all(value, "row", 0, 0, tiled=True)


def body(offsets, measured, block_brick, block_count):
    row = lax.axis_index("row")
    col = lax.axis_index("col")
    packed, residual = call(
        pack_kernel, (shape(8, 8, 1024), shape(3, 1024)), [VMEM, VMEM, SMEM, SMEM], traffic=1e6, out_specs=(VMEM, VMEM)
    )(offsets, measured, block_brick, block_count)
    points = lax.all_to_all(packed, "col", 0, 0, tiled=True)
    bricks = points[:, 6, ::128].reshape(64).astype(jnp.int32)
    meta = jnp.concatenate([bricks, jnp.stack([row, col]).astype(jnp.int32)])
    y_table = table_y()
    x_table = table_x()
    forward_y = jnp.asarray(halves(y_table))
    inverse_y = jnp.asarray(halves(y_table.transpose(0, 2, 1)))
    forward_x = jnp.asarray(halves(x_table))
    inverse_x = jnp.asarray(halves(x_table.transpose(0, 2, 1)))

    eight = pltpu.SemaphoreType.DMA((8,))
    scratch = [
        pltpu.VMEM((3, 1032, 256), F32),
        pltpu.VMEM((8, 256, 384), F32),
        pltpu.VMEM((4, 12, 1024), F32),
        TABLE,
        BLOCKS,
        eight,
        eight,
    ]
    sent, depth = call(
        first_spread_kernel,
        (shape(16, 392, 128), shape(64, 8, 128)),
        [SMEM, VMEM, ANY],
        scratch,
        40e6,
        (ANY, VMEM),
    )(meta, points, forward_y)
    received = [exchange(sent)]
    sent = call(
        functools.partial(spread_kernel, 1), shape(16, 392, 128), [SMEM, VMEM, ANY, VMEM], scratch, 40e6, ANY, 48
    )(meta, points, forward_y, depth)
    received.append(exchange(sent))
    spectra = []
    norms = []
    for pair in range(2):
        spectrum, sent, norm = call(
            functools.partial(spectrum_kernel, pair),
            (shape(2, 3, 2, 64, 1024), shape(16, 392, 128), shape(8, 128)),
            [SMEM, ANY, VMEM, VMEM],
            [
                pltpu.VMEM((8, 384, 256), F32),
                pltpu.VMEM((8, 384, 256), F32),
                pltpu.VMEM((128, 128), F32),
                BLOCKS,
                pltpu.SemaphoreType.DMA((4,)),
            ],
            40e6,
            (VMEM, VMEM, VMEM),
            40,
        )(meta, received[pair], forward_x, inverse_x)
        spectra.append(spectrum)
        norms.append(norm)
        received[pair] = exchange(sent)
    scratch = [
        pltpu.VMEM((3, 1040, 256), BF16),
        pltpu.VMEM((3, 1040, 256), BF16),
        pltpu.VMEM((8, 256, 384), F32),
        pltpu.VMEM((8, 6, 256), F32),
        pltpu.VMEM((4, 12, 1024), F32),
        TABLE,
        BLOCKS,
        eight,
        eight,
    ]
    velocity = call(first_gather_kernel, shape(8, 24, 128), [SMEM, VMEM, VMEM, ANY, ANY], scratch, 40e6, VMEM, 48)(
        meta, points, depth, received[0], inverse_y
    )
    velocity = call(
        functools.partial(gather_kernel, 1), shape(8, 24, 128), [SMEM, VMEM, VMEM, VMEM, ANY, ANY], scratch, 40e6
    )(meta, points, depth, velocity, received[1], inverse_y)
    velocity = lax.all_to_all(velocity, "col", 0, 0, tiled=True)
    velocity, sums = call(sums_kernel, (shape(3, 1024), shape(16, 8, 128)), [SMEM] + [VMEM] * 3, traffic=1e6, out_specs=(VMEM, VMEM))(
        block_count, velocity, *norms
    )
    sums = lax.all_to_all(sums, "row", 0, 0, tiled=True)
    sums = spread_out(jnp.sum(sums, axis=0), "col")
    twelve = pltpu.SemaphoreType.DMA((12,))
    return call(
        final_kernel,
        (shape(2, 3, 4, 64, 1024), shape(3, 1024)),
        [VMEM, VMEM, VMEM, ANY, ANY],
        [pltpu.VMEM((12, 2, 64, 1024), F32), twelve, twelve],
        13e6,
        (ANY, VMEM),
    )(sums, residual, velocity, *spectra)


def solution(mesh):
    in_specs = (
        P(None, ("row", "col")),
        P(None, ("row", "col")),
        P(("row", "col")),
        P(("row", "col")),
    )
    out_specs = (P(None, None, "col", "row", None), P(None, ("row", "col")))
    return jax.shard_map(body, mesh=mesh, in_specs=in_specs, out_specs=out_specs, check_vma=False)
```

```python
import functools
import math

import jax
import jax.numpy as jnp
import ml_dtypes
import numpy as np
from jax import lax
from jax.experimental import pallas as pl
from jax.experimental.pallas import tpu as pltpu
from jax.sharding import PartitionSpec as P

NX = 1024
NY = 1024
NZ = 64
CELLS = float(NX * NY * NZ)
TWO_PI = 2.0 * math.pi
F32 = jnp.float32
BF16 = jnp.bfloat16
VMEM_LIMIT = 64 * 1024 * 1024
VMEM = pl.BlockSpec(memory_space=pltpu.VMEM)
SMEM = pl.BlockSpec(memory_space=pltpu.SMEM)
ANY = pl.BlockSpec(memory_space=pl.ANY)
TABLE = pltpu.VMEM((8, 2, 256, 256), BF16)
BLOCKS = pltpu.VMEM((16, 784, 128), F32)


def halves(table):
    table = table.astype(np.float32)
    high = table.astype(ml_dtypes.bfloat16)
    low = (table - high.astype(np.float32)).astype(ml_dtypes.bfloat16)
    return np.stack([high, low], 1)


def table_y():
    first = np.arange(8)[:, None, None]
    angle = TWO_PI * ((np.arange(128)[None, :, None] * 8 + first) * np.arange(128)[None, None, :] % 1024) / 1024
    cosine, sine = np.cos(angle), np.sin(angle)
    return np.concatenate([np.concatenate([cosine, sine], 2), np.concatenate([-sine, cosine], 2)], 1)


def table_x():
    result = np.zeros((8, 2, 2, 64, 2, 64, 2))
    inner = np.arange(64)
    for first in range(8):
        for upper in range(2):
            wave = 16 * np.arange(64) + first + 8 * upper
            angle = TWO_PI * (inner[:, None] * wave[None, :] % 1024) / 1024
            result[first, upper, 0, :, 0, :, upper] = np.cos(angle)
            result[first, upper, 1, :, 0, :, upper] = np.sin(angle)
            result[first, upper, 0, :, 1, :, upper] = -np.sin(angle)
            result[first, upper, 1, :, 1, :, upper] = np.cos(angle)
    return result.reshape(8, 256, 256)


def table_edge():
    place = np.arange(128)
    result = np.zeros((8, 128, 2, 128))
    for first in range(8):
        for source in range(16):
            angle = TWO_PI * ((source + 1) * (first + 8 * (place % 2)) % 16) / 16
            result[first, 2 * source, 0] = np.cos(angle)
            result[first, 2 * source, 1] = -np.sin(angle)
            result[first, 2 * source + 1, 0] = np.sin(angle)
            result[first, 2 * source + 1, 1] = np.cos(angle)
    return result.reshape(8, 128, 256)


def stacked(table):
    high, low = table[:, 0, :32], table[:, 1, :32]
    return np.concatenate([high, high, low, np.zeros_like(low)], 1)


def split(value):
    high = value.astype(BF16)
    return high, (value - high.astype(F32)).astype(BF16)


def mul(left, right):
    return jnp.dot(left, right, preferred_element_type=F32)


def mul_t(left, right):
    return lax.dot_general(left, right, (((1,), (1,)), ((), ())), preferred_element_type=F32)


def doubled(high, low):
    return jnp.concatenate(
        [jnp.concatenate([high, high], 1), jnp.concatenate([low, jnp.zeros_like(low)], 1)], 0
    )


def small_dft(values, sign):
    count = len(values)
    if count == 1:
        return values
    even = small_dft(values[0::2], sign)
    odd = small_dft(values[1::2], sign)
    low, high = [], []
    for k in range(count // 2):
        real, imag = odd[k]
        if k > 0:
            if 4 * k == count:
                real, imag = (-imag, real) if sign > 0 else (imag, -real)
            elif 8 * k == count:
                root = math.sqrt(0.5)
                if sign > 0:
                    real, imag = (real - imag) * root, (real + imag) * root
                else:
                    real, imag = (real + imag) * root, (imag - real) * root
            elif 8 * k == 3 * count:
                root = math.sqrt(0.5)
                if sign > 0:
                    real, imag = (real + imag) * -root, (real - imag) * root
                else:
                    real, imag = (imag - real) * root, (real + imag) * -root
            else:
                cosine = math.cos(TWO_PI * k / count)
                sine = sign * math.sin(TWO_PI * k / count)
                real, imag = real * cosine - imag * sine, real * sine + imag * cosine
        low.append((even[k][0] + real, even[k][1] + imag))
        high.append((even[k][0] - real, even[k][1] - imag))
    return low + high


def hat(distance):
    return jnp.maximum(1.0 - jnp.abs(distance), 0.0)


def ramp(shape, axis):
    return lax.broadcasted_iota(jnp.int32, shape, axis).astype(F32)


def brick_place(brick):
    return brick // 64, brick // 2 % 32, brick % 2


def block_points(points, block):
    lane = pl.multiple_of(block % 8 * 128, 128)
    return points[block // 8, :, pl.ds(lane, 128)]


def depth_waves(meta, block, point):
    index = lax.broadcasted_iota(jnp.int32, (8, 128), 0)
    mode = 4 * meta[65] + 2 * (index // 4) + index % 2
    turn = 16 * (index // 2 % 2)

    def wave(cell):
        angle = (mode * cell + turn) & 63
        value = (jnp.abs(angle - 32) - 16).astype(F32) * (math.pi / 32.0)
        square = value * value
        total = -1.0 / 39916800.0
        for factor in (1.0 / 362880.0, -1.0 / 5040.0, 1.0 / 120.0, -1.0 / 6.0, 1.0):
            total = total * square + factor
        return total * value

    lower = jnp.floor(point[2:3])
    part = point[2:3] - lower
    cell = lower.astype(jnp.int32) + 32 * (meta[block] % 2)
    return (1.0 - part) * wave(cell) + part * wave(cell + 1)


def edge_weights(along):
    return jnp.concatenate([along[:40], jnp.zeros((88, 128), F32)], 0)


def edge_waves(point, waves, place_x):
    return waves * jnp.maximum(point[0:1] - (63 - 32 * place_x).astype(F32), 0.0)


def lower_lanes(rows):
    return lax.broadcasted_iota(jnp.int32, (rows, 128), 1) < 64


def joined(first, second):
    lower = lower_lanes(first.shape[0])
    return (
        jnp.where(lower, first, pltpu.roll(second, 64, 1)),
        jnp.where(lower, pltpu.roll(first, 64, 1), second),
    )


def pack_kernel(offsets, measured, bricks, counts, out, residual):
    lane = lax.broadcasted_iota(jnp.int32, (3, 128), 1)
    for i in range(8):
        at = slice(128 * i, 128 * i + 128)
        residual[:, at] = jnp.where(lane < counts[i], measured[:, at], 0.0)
        brick = jnp.zeros((2, 128), F32) + bricks[i].astype(F32)
        block = jnp.concatenate([offsets[:, at], residual[:, at], brick], 0)
        for dest in range(8):
            out[dest, :, at] = block


def slab_weights(point, waves, place_x):
    across = hat(ramp((64, 128), 0) - (32 * place_x).astype(F32) - point[0:1])
    return jnp.concatenate([waves[i : i + 1] * across for i in range(8)], 0)


def spread_kernel(
    meta, points, far_table, far_out, depth, field, parts, windows, table, out, table_done, out_done
):
    def table_copy(k):
        return pltpu.make_async_copy(far_table.at[k], table.at[k], table_done.at[k])

    def out_copy(k):
        at = pl.ds(2 * k, 2)
        return pltpu.make_async_copy(out.at[at], far_out.at[at], out_done.at[k])

    for k in range(8):
        table_copy(k).start()
    field[...] = jnp.zeros_like(field)
    windows[...] = jnp.zeros_like(windows)

    def step(block, carry):
        place_x, place_y, _ = brick_place(meta[block])
        point = block_points(points, block)
        waves = depth_waves(meta, block, point)
        depth[block] = waves
        weight_high, weight_low = split(slab_weights(point, waves, place_x))
        along = hat(ramp((40, 128), 0) - point[1:2])
        source = jnp.concatenate([along * point[3 + c : 4 + c] for c in range(3)], 0)
        both = mul_t(doubled(*split(source)), jnp.concatenate([weight_high, weight_low], 1))
        value = both[:120] + both[120:]
        row = pl.multiple_of(place_y * 32, 32)
        for c in range(3):
            field[c, pl.ds(row, 40), :] += value[40 * c : 40 * c + 40]
        waves = edge_waves(point, waves, place_x)
        source = jnp.concatenate([waves[i : i + 1] * point[3:6] for i in range(8)], 0)
        both = mul_t(doubled(*split(source)), jnp.concatenate(split(edge_weights(along)), 1))
        lane = pl.multiple_of(place_y // 4 * 128, 128)
        windows[place_y % 4, :, pl.ds(lane, 128)] += both[:24] + both[24:]
        return carry

    lax.fori_loop(0, 64, step, 0, unroll=32)
    for c in range(3):
        field[c, 0:1, :] += field[c, 1024:1025, :]

    def outer(tile, carry):
        row = pl.multiple_of(tile * 8, 8)
        for c in range(3):
            for p in range(2):
                lane = 256 * p
                values = [
                    (
                        field[c, pl.ds(128 * a + row, 8), lane : lane + 128],
                        field[c, pl.ds(128 * a + row, 8), lane + 128 : lane + 256],
                    )
                    for a in range(8)
                ]
                to = 128 * (3 * p + c)
                for k, (real, imag) in enumerate(small_dft(values, -1)):
                    parts[k, pl.ds(row, 8), to : to + 128] = real
                    parts[k, pl.ds(128 + row, 8), to : to + 128] = imag
        return carry

    lax.fori_loop(0, 16, outer, 0, unroll=4)
    total = windows[0]
    for j in range(1, 4):
        total = total + pltpu.roll(windows[j], 32 * j, 1)
    real = jnp.concatenate([total[0:6], total[12:18]], 0)
    imag = jnp.concatenate([total[6:12], total[18:24]], 0)
    values = [(real[:, 128 * a : 128 * a + 128], imag[:, 128 * a : 128 * a + 128]) for a in range(8)]
    for k, pieces in enumerate(small_dft(values, -1)):
        windows[k // 2, 0:12, 256 * (k % 2) : 256 * (k % 2) + 256] = jnp.concatenate(pieces, 1)

    def inner(k, carry):
        table_copy(k).wait()
        high, low = split(parts[k])
        value = mul(table[k, 0], high) + mul(table[k, 1], high) + mul(table[k, 0], low)
        high, low = split(windows[k // 2, 0:12, pl.ds(pl.multiple_of(256 * (k % 2), 256), 256)])
        edge = mul_t(high, table[k, 0]) + mul_t(high, table[k, 1]) + mul_t(low, table[k, 0])
        for p in range(2):
            rows = edge[6 * p : 6 * p + 6]
            sides = [joined(rows[0:3, at : at + 128], rows[3:6, at : at + 128]) for at in (0, 128)]
            for half in range(2):
                for c in range(3):
                    for part in range(2):
                        row = 128 * part + 64 * half
                        to = 392 * p + 64 * (2 * c + part)
                        at = 128 * (3 * p + c)
                        out[2 * k + half, to : to + 64] = value[row : row + 64, at : at + 128]
                out[2 * k + half, 392 * p + 384 : 392 * p + 392] = jnp.concatenate(
                    [sides[part][half][c : c + 1] for c in range(3) for part in range(2)]
                    + [jnp.zeros((2, 128), F32)],
                    0,
                )
        out_copy(k).start()
        return carry

    lax.fori_loop(0, 8, inner, 0)
    for k in range(8):
        out_copy(k).wait()


def spectrum_kernel(
    meta, far_received, far_table, far_back, edge_table, edge_stack, far_spectrum, far_out, norm,
    received, out, spectrum, parts, back, edge_sum, table, table_back,
    received_done, out_done, spectrum_done, table_done, back_done,
):
    row = meta[64]

    def place(p, c):
        return pl.ds(392 * p + 128 * c, 128 if c < 3 else 8)

    def received_copy(p, c):
        at = place(p, c)
        return pltpu.make_async_copy(far_received.at[:, at], received.at[:, at], received_done.at[4 * p + c])

    def out_copy(p, c):
        at = place(p, c)
        return pltpu.make_async_copy(out.at[:, at], far_out.at[:, at], out_done.at[4 * p + c])

    def spectrum_copy(p, part):
        to = far_spectrum.at[part, :, pl.ds(2 * p, 2)]
        return pltpu.make_async_copy(spectrum.at[p, part], to, spectrum_done.at[2 * p + part])

    def table_copy(k):
        return pltpu.make_async_copy(far_table.at[k], table.at[k], table_done.at[k])

    def back_copy(k):
        return pltpu.make_async_copy(far_back.at[k], table_back.at[k], back_done.at[k])

    for c in (3, 0, 1, 2):
        received_copy(0, c).start()
    for k in range(8):
        table_copy(k).start()
        back_copy(k).start()
    for c in (3, 0, 1, 2):
        received_copy(1, c).start()

    index_y = 8 * (64 * (row % 2) + lax.broadcasted_iota(jnp.int32, (64, 128), 0)) + row // 2
    lane_x = lax.broadcasted_iota(jnp.int32, (64, 128), 1)
    wave_y = jnp.where(index_y < NY // 2, index_y, index_y - NY).astype(F32) * (TWO_PI / NY)
    sums = jnp.zeros((64, 128), F32)
    for p in range(2):
        base = 392 * p

        def outer(c, tile, carry):
            at = pl.multiple_of(tile * 8, 8)
            first = base + 128 * c
            values = [
                (received[s, pl.ds(first + at, 8)], received[s, pl.ds(first + 64 + at, 8)]) for s in range(16)
            ]
            for k, (real, imag) in enumerate(small_dft(values, -1)):
                to = 128 * (k // 8)
                first, second = joined(real, imag)
                parts[k % 8, pl.ds(128 * c + at, 8), to : to + 128] = first
                parts[k % 8, pl.ds(128 * c + 64 + at, 8), to : to + 128] = second
            return carry

        for c in range(3):
            received_copy(p, c).wait()
            lax.fori_loop(0, 8, functools.partial(outer, c), 0, unroll=8)
        received_copy(p, 3).wait()
        columns = []
        for c in range(3):
            at = base + 384 + 2 * c
            rows = jnp.concatenate([received[s, at : at + 2] for s in range(16)], 0)
            high = rows.astype(BF16).astype(F32)
            columns.append(jnp.concatenate([high, rows - high, high, jnp.zeros((32, 128), F32)], 0).T.astype(BF16))
        edge = jnp.concatenate(columns, 0)
        edge_sum[...] = jnp.zeros_like(edge_sum)

        def inner(k, total):
            if p == 0:
                table_copy(k).wait()
                back_copy(k).wait()
            high, low = split(parts[k])
            value = mul(high, table[k, 0]) + mul(low, table[k, 0]) + mul(high, table[k, 1])
            value = value + mul(edge, edge_stack[k])
            index_x = 8 * lane_x + k
            wave_x = jnp.where(index_x < NX // 2, index_x, index_x - NX).astype(F32) * (TWO_PI / NX)
            flat = wave_x * wave_x + wave_y * wave_y
            valid = (index_y != NY // 2) & (index_x != NX // 2)
            to = pl.multiple_of(k * 128, 128)
            rows = [[None, None] for _ in range(3)]
            for h in range(2):
                index_z = 4 * meta[65] + 2 * p + h
                wave_z = index_z.astype(F32) * (TWO_PI / NZ)
                weight = jnp.where(index_z == 0, 1.0, 2.0).astype(F32) / CELLS
                squared = flat + wave_z * wave_z
                keep = valid & (squared > 0.0)
                inverse = jnp.where(keep, 1.0 / jnp.where(keep, squared, 1.0), 0.0)

                def crossed(vector, scale):
                    return [
                        (wave_y * vector[2] - wave_z * vector[1]) * scale,
                        (wave_z * vector[0] - wave_x * vector[2]) * scale,
                        (wave_x * vector[1] - wave_y * vector[0]) * scale,
                    ]

                start = [128 * c + 64 * h for c in range(3)]
                real = [value[s : s + 64, 0:128] for s in start]
                imag = [value[s : s + 64, 128:256] for s in start]
                grad_real = crossed(imag, -inverse)
                grad_imag = crossed(real, inverse)
                square = 0.0
                for c in range(3):
                    spectrum[p, 0, c, h, :, pl.ds(to, 128)] = grad_real[c]
                    spectrum[p, 1, c, h, :, pl.ds(to, 128)] = grad_imag[c]
                    square = square + grad_real[c] * grad_real[c] + grad_imag[c] * grad_imag[c]
                total = total + weight * square
                scale = inverse * weight
                back_real = crossed(grad_imag, -scale)
                back_imag = crossed(grad_real, scale)
                for c in range(3):
                    rows[c][h] = jnp.concatenate([back_real[c], back_imag[c]], 1)
            high, low = split(jnp.concatenate([rows[c][h] for c in range(3) for h in range(2)], 0))
            back[k] = mul(high, table_back[k, 0]) + mul(low, table_back[k, 0]) + mul(high, table_back[k, 1])
            edge_sum[...] += (
                mul_t(high, edge_table[k, 0]) + mul_t(high, edge_table[k, 1]) + mul_t(low, edge_table[k, 0])
            )
            return total

        sums = lax.fori_loop(0, 8, inner, sums, unroll=8)
        for part in range(2):
            spectrum_copy(p, part).start()

        def last(c, tile, carry):
            at = pl.multiple_of(tile * 8, 8)
            values = []
            for k in range(16):
                to = 128 * (k // 8)
                first = back[k % 8, pl.ds(128 * c + at, 8), to : to + 128]
                second = back[k % 8, pl.ds(128 * c + 64 + at, 8), to : to + 128]
                values.append(joined(first, second))
            for s, pieces in enumerate(small_dft(values, 1)):
                for part in range(2):
                    out[s, pl.ds(base + 128 * c + 64 * part + at, 8)] = pieces[part]
            return carry

        turned = [edge_sum[128 * c : 128 * c + 128, :].T for c in range(3)]
        for s in range(16):
            out[s, base + 384 : base + 392] = jnp.concatenate(
                [turned[c][2 * s : 2 * s + 2] for c in range(3)] + [jnp.zeros((2, 128), F32)], 0
            )
        out_copy(p, 3).start()
        for c in range(3):
            lax.fori_loop(0, 8, functools.partial(last, c), 0, unroll=8)
            out_copy(p, c).start()
    norm[...] = jnp.sum(sums.reshape(8, 8, 128), axis=0)
    for p in range(2):
        for part in range(2):
            spectrum_copy(p, part).wait()
        for c in range(4):
            out_copy(p, c).wait()


def gather_kernel(
    meta, points, depth, far_received, far_table, out,
    field_high, field_low, parts, edge, windows, table, received, table_done, received_done,
):
    def table_copy(k):
        return pltpu.make_async_copy(far_table.at[k], table.at[k], table_done.at[k])

    def received_copy(k):
        at = pl.ds(2 * k, 2)
        return pltpu.make_async_copy(far_received.at[at], received.at[at], received_done.at[k])

    for k in range(8):
        table_copy(k).start()
        received_copy(k).start()

    def inner(k, carry):
        table_copy(k).wait()
        received_copy(k).wait()
        columns = []
        for p in range(2):
            for c in range(3):
                pieces = []
                for part in range(2):
                    for half in range(2):
                        at = 392 * p + 64 * (2 * c + part)
                        pieces.append(received[2 * k + half, at : at + 64])
                columns.append(jnp.concatenate(pieces, 0))
        high, low = split(jnp.concatenate(columns, 1))
        parts[k] = mul(table[k, 0], high) + mul(table[k, 1], high) + mul(table[k, 0], low)
        sides = []
        for p in range(2):
            at = 392 * p + 384
            sides.append(joined(received[2 * k, at : at + 8], received[2 * k + 1, at : at + 8]))
        rows = [
            jnp.concatenate(
                [sides[p][h][2 * c + part : 2 * c + part + 1] for p in range(2) for h in range(2) for c in range(3)],
                0,
            )
            for part in range(2)
        ]
        high, low = split(jnp.concatenate(rows, 1))
        edge[k] = mul_t(high, table[k, 0]) + mul_t(high, table[k, 1]) + mul_t(low, table[k, 0])
        return carry

    lax.fori_loop(0, 8, inner, 0)
    values = [(edge[k, :, 0:128], edge[k, :, 128:256]) for k in range(8)]
    planes = []
    for real, imag in small_dft(values, 1):
        planes.append(jnp.concatenate([real[0:6], imag[0:6], real[6:12], imag[6:12]], 0))
    plane = jnp.concatenate(planes, 1)
    for j in range(4):
        windows[j] = plane if j == 0 else pltpu.roll(plane, 1024 - 32 * j, 1)

    def outer(tile, carry):
        row = pl.multiple_of(tile * 16, 16)
        for c in range(3):
            for p in range(2):
                at = 128 * (3 * p + c)
                values = [
                    (parts[k, pl.ds(row, 16), at : at + 128], parts[k, pl.ds(128 + row, 16), at : at + 128])
                    for k in range(8)
                ]
                for a, pieces in enumerate(small_dft(values, 1)):
                    for part in range(2):
                        high, low = split(pieces[part])
                        lane = 256 * p + 128 * part
                        field_high[c, pl.ds(128 * a + row, 16), lane : lane + 128] = high
                        field_low[c, pl.ds(128 * a + row, 16), lane : lane + 128] = low
        return carry

    lax.fori_loop(0, 8, outer, 0)
    for c in range(3):
        field_high[c, 1024:1040, :] = field_high[c, 0:16, :]
        field_low[c, 1024:1040, :] = field_low[c, 0:16, :]

    def step(block, carry):
        place_x, place_y, _ = brick_place(meta[block])
        point = block_points(points, block)
        waves = depth[block]
        weight_high, weight_low = split(slab_weights(point, waves, place_x))
        along = hat(ramp((48, 128), 0) - point[1:2])
        row = pl.multiple_of(place_y * 32, 32)
        high = jnp.concatenate([field_high[c, pl.ds(row, 48), :] for c in range(3)], 0)
        low = jnp.concatenate([field_low[c, pl.ds(row, 48), :] for c in range(3)], 0)
        both = mul(high, jnp.concatenate([weight_high, weight_low], 1))
        value = both[:, :128] + both[:, 128:] + mul(low, weight_high)
        velocity = [jnp.sum(along * value[48 * c : 48 * c + 48], axis=0, keepdims=True) for c in range(3)]
        waves = edge_waves(point, waves, place_x)
        weight_high, weight_low = split(edge_weights(along))
        lane = pl.multiple_of(place_y // 4 * 128, 128)
        high, low = split(windows[place_y % 4, :, pl.ds(lane, 128)])
        value = mul(high, weight_high) + mul(low, weight_high) + mul(high, weight_low)
        more = sum(waves[i : i + 1] * value[3 * i : 3 * i + 3] for i in range(8))
        for c in range(3):
            out[block // 8, pl.ds(8 * c + block % 8, 1), :] = velocity[c] + more[c : c + 1]
        return carry

    lax.fori_loop(0, 64, step, 0, unroll=32)


def sums_kernel(counts, received, norms, velocity, out):
    row = lax.broadcasted_iota(jnp.int32, (8, 128), 0)
    count = jnp.zeros((8, 128), jnp.int32)
    for i in range(8):
        count = jnp.where(row == i, counts[i], count)
    live = lax.broadcasted_iota(jnp.int32, (8, 128), 1) < count
    square = jnp.zeros((8, 128), F32)
    for c in range(3):
        total = received[0, 8 * c : 8 * c + 8]
        for source in range(1, 8):
            total = total + received[source, 8 * c : 8 * c + 8]
        total = jnp.where(live, total, 0.0)
        square = square + total * total
        for i in range(8):
            velocity[c : c + 1, 128 * i : 128 * i + 128] = total[i : i + 1]
    norm = jnp.sum(norms[...], axis=0, keepdims=True)
    square = jnp.sum(square, axis=0, keepdims=True)
    tile = jnp.where(row == 0, norm, jnp.where(row == 1, square, 0.0))
    for dest in range(16):
        out[dest] = tile


def final_kernel(sums, residual, velocity, gradient, spectrum, out, values, loaded, stored):
    def load(i):
        source = gradient.at[i // 6, i // 2 % 3, pl.ds(i % 2 * 2, 2)]
        return pltpu.make_async_copy(source, values.at[i], loaded.at[i])

    def store(i):
        place = spectrum.at[i // 6, i // 2 % 3, pl.ds(i % 2 * 2, 2)]
        return pltpu.make_async_copy(values.at[i], place, stored.at[i])

    for i in range(12):
        load(i).start()
    total = jnp.sum(jnp.sum(sums[...], axis=0), axis=1, keepdims=True)
    length = total[0:1] / total[1:2]
    scale = length * (1.0 / math.sqrt(CELLS))
    for i in range(12):
        load(i).wait()
        values[i] = values[i] * scale
        store(i).start()
    out[...] = residual[...] - length * velocity[...]
    for i in range(12):
        store(i).wait()


def call(kernel, outs, specs, scratch=(), traffic=0, out_specs=VMEM):
    return pl.pallas_call(
        kernel,
        out_shape=outs,
        in_specs=specs,
        out_specs=out_specs,
        scratch_shapes=list(scratch),
        cost_estimate=pl.CostEstimate(flops=0, bytes_accessed=int(traffic), transcendentals=0),
        compiler_params=pltpu.CompilerParams(vmem_limit_bytes=VMEM_LIMIT),
    )


def near(value):
    return pltpu.with_memory_space_constraint(value, pltpu.VMEM)


def far(value):
    return pltpu.with_memory_space_constraint(value, pltpu.HBM)


def near_shape(*dims):
    return pltpu.VMEM(dims, F32)


def shape(*dims):
    return jax.ShapeDtypeStruct(dims, F32)


def spread_out(value, axis):
    count = lax.axis_size(axis)
    return lax.all_to_all(jnp.broadcast_to(value[None], (count,) + value.shape), axis, 0, 0, tiled=True)


def exchange(value):
    return lax.all_to_all(value, "row", 0, 0, tiled=True)


def body(offsets, measured, block_brick, block_count):
    row = lax.axis_index("row")
    col = lax.axis_index("col")
    packed, residual = call(
        pack_kernel, (shape(8, 8, 1024), shape(3, 1024)), [VMEM, VMEM, SMEM, SMEM], traffic=1e6, out_specs=(VMEM, VMEM)
    )(offsets, measured, block_brick, block_count)
    points = lax.all_to_all(packed, "col", 0, 0, tiled=True)
    bricks = points[:, 6, ::128].reshape(64).astype(jnp.int32)
    meta = jnp.concatenate([bricks, jnp.stack([row, col]).astype(jnp.int32)])
    y_table = table_y()
    x_table = table_x()
    forward_y = jnp.asarray(halves(y_table))
    inverse_y = jnp.asarray(halves(y_table.transpose(0, 2, 1)))
    forward_x = jnp.asarray(halves(x_table))
    inverse_x = jnp.asarray(halves(x_table.transpose(0, 2, 1)))

    edge_table = halves(table_edge())
    eight = pltpu.SemaphoreType.DMA((8,))
    sent, depth = call(
        spread_kernel,
        (shape(16, 784, 128), shape(64, 8, 128)),
        [SMEM, VMEM, ANY],
        [
            pltpu.VMEM((3, 1032, 512), F32),
            pltpu.VMEM((8, 256, 768), F32),
            pltpu.VMEM((4, 24, 1024), F32),
            TABLE,
            BLOCKS,
            eight,
            eight,
        ],
        40e6,
        (ANY, VMEM),
    )(meta, points, forward_y)
    received = exchange(sent)
    spectrum, sent, norm = call(
        spectrum_kernel,
        (shape(2, 3, 4, 64, 1024), shape(16, 784, 128), shape(8, 128)),
        [SMEM, ANY, ANY, ANY, VMEM, VMEM],
        [
            BLOCKS,
            BLOCKS,
            pltpu.VMEM((2, 2, 3, 2, 64, 1024), F32),
            pltpu.VMEM((8, 384, 256), F32),
            pltpu.VMEM((8, 384, 256), F32),
            pltpu.VMEM((384, 128), F32),
            TABLE,
            TABLE,
            eight,
            eight,
            pltpu.SemaphoreType.DMA((4,)),
            eight,
            eight,
        ],
        40e6,
        (ANY, ANY, VMEM),
    )(meta, received, forward_x, inverse_x, jnp.asarray(edge_table), jnp.asarray(stacked(edge_table)))
    received = exchange(sent)
    velocity = call(
        gather_kernel,
        shape(8, 24, 128),
        [SMEM, VMEM, VMEM, ANY, ANY],
        [
            pltpu.VMEM((3, 1040, 512), BF16),
            pltpu.VMEM((3, 1040, 512), BF16),
            pltpu.VMEM((8, 256, 768), F32),
            pltpu.VMEM((8, 12, 256), F32),
            pltpu.VMEM((4, 24, 1024), F32),
            TABLE,
            BLOCKS,
            eight,
            eight,
        ],
        40e6,
    )(meta, points, depth, received, inverse_y)
    velocity = lax.all_to_all(velocity, "col", 0, 0, tiled=True)
    velocity, sums = call(sums_kernel, (shape(3, 1024), shape(16, 8, 128)), [SMEM] + [VMEM] * 2, traffic=1e6, out_specs=(VMEM, VMEM))(
        block_count, velocity, norm
    )
    sums = lax.all_to_all(sums, "row", 0, 0, tiled=True)
    sums = spread_out(jnp.sum(sums, axis=0), "col")
    twelve = pltpu.SemaphoreType.DMA((12,))
    return call(
        final_kernel,
        (shape(2, 3, 4, 64, 1024), shape(3, 1024)),
        [VMEM, VMEM, VMEM, ANY],
        [pltpu.VMEM((12, 2, 64, 1024), F32), twelve, twelve],
        13e6,
        (ANY, VMEM),
    )(sums, residual, velocity, spectrum)


def solution(mesh):
    in_specs = (
        P(None, ("row", "col")),
        P(None, ("row", "col")),
        P(("row", "col")),
        P(("row", "col")),
    )
    out_specs = (P(None, None, "col", "row", None), P(None, ("row", "col")))
    return jax.shard_map(body, mesh=mesh, in_specs=in_specs, out_specs=out_specs, check_vma=False)
```

```python
import functools
import math

import jax
import jax.numpy as jnp
import ml_dtypes
import numpy as np
from jax import lax
from jax.experimental import pallas as pl
from jax.experimental.pallas import tpu as pltpu
from jax.sharding import PartitionSpec as P

NX = 1024
NY = 1024
NZ = 64
CELLS = float(NX * NY * NZ)
TWO_PI = 2.0 * math.pi
F32 = jnp.float32
BF16 = jnp.bfloat16
VMEM_LIMIT = 64 * 1024 * 1024
LIM_A = 44 * 1024 * 1024
LIM_X = 36 * 1024 * 1024
VMEM = pl.BlockSpec(memory_space=pltpu.VMEM)
SMEM = pl.BlockSpec(memory_space=pltpu.SMEM)
ANY = pl.BlockSpec(memory_space=pl.ANY)
TABLE = pltpu.VMEM((8, 2, 256, 256), BF16)


def halves(table):
    table = table.astype(np.float32)
    high = table.astype(ml_dtypes.bfloat16)
    low = (table - high.astype(np.float32)).astype(ml_dtypes.bfloat16)
    return np.stack([high, low], 1)


def table_y():
    first = np.arange(8)[:, None, None]
    angle = TWO_PI * ((np.arange(128)[None, :, None] * 8 + first) * np.arange(128)[None, None, :] % 1024) / 1024
    cosine, sine = np.cos(angle), np.sin(angle)
    return np.concatenate([np.concatenate([cosine, sine], 2), np.concatenate([-sine, cosine], 2)], 1)


def table_x():
    result = np.zeros((8, 2, 2, 64, 2, 64, 2))
    inner = np.arange(64)
    for first in range(8):
        for upper in range(2):
            wave = 16 * np.arange(64) + first + 8 * upper
            angle = TWO_PI * (inner[:, None] * wave[None, :] % 1024) / 1024
            result[first, upper, 0, :, 0, :, upper] = np.cos(angle)
            result[first, upper, 1, :, 0, :, upper] = np.sin(angle)
            result[first, upper, 0, :, 1, :, upper] = -np.sin(angle)
            result[first, upper, 1, :, 1, :, upper] = np.cos(angle)
    return result.reshape(8, 256, 256)


def table_edge():
    place = np.arange(128)
    result = np.zeros((8, 128, 2, 128))
    for first in range(8):
        for source in range(16):
            angle = TWO_PI * ((source + 1) * (first + 8 * (place % 2)) % 16) / 16
            result[first, 2 * source, 0] = np.cos(angle)
            result[first, 2 * source, 1] = -np.sin(angle)
            result[first, 2 * source + 1, 0] = np.sin(angle)
            result[first, 2 * source + 1, 1] = np.cos(angle)
    return result.reshape(8, 128, 256)


def stacked(table):
    high, low = table[:, 0, :32], table[:, 1, :32]
    return np.concatenate([high, high, low, np.zeros_like(low)], 1)


def split(value):
    high = value.astype(BF16)
    return high, (value - high.astype(F32)).astype(BF16)


def mul(left, right):
    return jnp.dot(left, right, preferred_element_type=F32)


def mul_t(left, right):
    return lax.dot_general(left, right, (((1,), (1,)), ((), ())), preferred_element_type=F32)


def doubled(high, low):
    return jnp.concatenate(
        [jnp.concatenate([high, high], 1), jnp.concatenate([low, jnp.zeros_like(low)], 1)], 0
    )


def small_dft(values, sign):
    count = len(values)
    if count == 1:
        return values
    even = small_dft(values[0::2], sign)
    odd = small_dft(values[1::2], sign)
    low, high = [], []
    for k in range(count // 2):
        real, imag = odd[k]
        if k > 0:
            if 4 * k == count:
                real, imag = (-imag, real) if sign > 0 else (imag, -real)
            elif 8 * k == count:
                root = math.sqrt(0.5)
                if sign > 0:
                    real, imag = (real - imag) * root, (real + imag) * root
                else:
                    real, imag = (real + imag) * root, (imag - real) * root
            elif 8 * k == 3 * count:
                root = math.sqrt(0.5)
                if sign > 0:
                    real, imag = (real + imag) * -root, (real - imag) * root
                else:
                    real, imag = (imag - real) * root, (real + imag) * -root
            else:
                cosine = math.cos(TWO_PI * k / count)
                sine = sign * math.sin(TWO_PI * k / count)
                real, imag = real * cosine - imag * sine, real * sine + imag * cosine
        low.append((even[k][0] + real, even[k][1] + imag))
        high.append((even[k][0] - real, even[k][1] - imag))
    return low + high


def hat(distance):
    return jnp.maximum(1.0 - jnp.abs(distance), 0.0)


def ramp(shape, axis):
    return lax.broadcasted_iota(jnp.int32, shape, axis).astype(F32)


def brick_place(brick):
    return brick // 64, brick // 2 % 32, brick % 2


def block_points(points, block):
    lane = pl.multiple_of(block % 8 * 128, 128)
    return points[block // 8, :, pl.ds(lane, 128)]


def depth_waves(meta, block, point):
    index = lax.broadcasted_iota(jnp.int32, (8, 128), 0)
    mode = 4 * meta[65] + 2 * (index // 4) + index % 2
    turn = 16 * (index // 2 % 2)

    def wave(cell):
        angle = (mode * cell + turn) & 63
        value = (jnp.abs(angle - 32) - 16).astype(F32) * (math.pi / 32.0)
        square = value * value
        total = -1.0 / 39916800.0
        for factor in (1.0 / 362880.0, -1.0 / 5040.0, 1.0 / 120.0, -1.0 / 6.0, 1.0):
            total = total * square + factor
        return total * value

    lower = jnp.floor(point[2:3])
    part = point[2:3] - lower
    cell = lower.astype(jnp.int32) + 32 * (meta[block] % 2)
    return (1.0 - part) * wave(cell) + part * wave(cell + 1)


def edge_weights(along):
    return jnp.concatenate([along[:40], jnp.zeros((88, 128), F32)], 0)


def edge_waves(point, waves, place_x):
    return waves * jnp.maximum(point[0:1] - (63 - 32 * place_x).astype(F32), 0.0)


def lower_lanes(rows):
    return lax.broadcasted_iota(jnp.int32, (rows, 128), 1) < 64


def joined(first, second):
    lower = lower_lanes(first.shape[0])
    return (
        jnp.where(lower, first, pltpu.roll(second, 64, 1)),
        jnp.where(lower, pltpu.roll(first, 64, 1), second),
    )


def pack_kernel(offsets, measured, bricks, counts, out, residual):
    lane = lax.broadcasted_iota(jnp.int32, (3, 128), 1)
    for i in range(8):
        at = slice(128 * i, 128 * i + 128)
        residual[:, at] = jnp.where(lane < counts[i], measured[:, at], 0.0)
        brick = jnp.zeros((2, 128), F32) + bricks[i].astype(F32)
        block = jnp.concatenate([offsets[:, at], residual[:, at], brick], 0)
        for dest in range(8):
            out[dest, :, at] = block


def slab_weights(point, waves, place_x):
    across = hat(ramp((64, 128), 0) - (32 * place_x).astype(F32) - point[0:1])
    return jnp.concatenate([waves[i : i + 1] * across for i in range(8)], 0)


def spread_kernel(
    meta, points, far_table, out, depth, field, parts, windows, table, table_done
):
    def table_copy(k):
        return pltpu.make_async_copy(far_table.at[k], table.at[k], table_done.at[k])

    for k in range(8):
        table_copy(k).start()
    field[...] = jnp.zeros_like(field)
    windows[...] = jnp.zeros_like(windows)

    def step(block, carry):
        place_x, place_y, _ = brick_place(meta[block])
        point = block_points(points, block)
        waves = depth_waves(meta, block, point)
        depth[block] = waves
        weight_high, weight_low = split(slab_weights(point, waves, place_x))
        along = hat(ramp((40, 128), 0) - point[1:2])
        source = jnp.concatenate([along * point[3 + c : 4 + c] for c in range(3)], 0)
        both = mul_t(doubled(*split(source)), jnp.concatenate([weight_high, weight_low], 1))
        value = both[:120] + both[120:]
        row = pl.multiple_of(place_y * 32, 32)
        for c in range(3):
            field[c, pl.ds(row, 40), :] += value[40 * c : 40 * c + 40]
        waves = edge_waves(point, waves, place_x)
        source = jnp.concatenate([waves[i : i + 1] * point[3:6] for i in range(8)], 0)
        both = mul_t(doubled(*split(source)), jnp.concatenate(split(edge_weights(along)), 1))
        lane = pl.multiple_of(place_y // 4 * 128, 128)
        windows[place_y % 4, :, pl.ds(lane, 128)] += both[:24] + both[24:]
        return carry

    lax.fori_loop(0, 64, step, 0, unroll=32)
    for c in range(3):
        field[c, 0:1, :] += field[c, 1024:1025, :]

    def outer(tile, carry):
        row = pl.multiple_of(tile * 8, 8)
        for c in range(3):
            for p in range(2):
                lane = 256 * p
                values = [
                    (
                        field[c, pl.ds(128 * a + row, 8), lane : lane + 128],
                        field[c, pl.ds(128 * a + row, 8), lane + 128 : lane + 256],
                    )
                    for a in range(8)
                ]
                to = 128 * (3 * p + c)
                for k, (real, imag) in enumerate(small_dft(values, -1)):
                    parts[k, pl.ds(row, 8), to : to + 128] = real
                    parts[k, pl.ds(128 + row, 8), to : to + 128] = imag
        return carry

    lax.fori_loop(0, 16, outer, 0, unroll=4)
    total = windows[0]
    for j in range(1, 4):
        total = total + pltpu.roll(windows[j], 32 * j, 1)
    real = jnp.concatenate([total[0:6], total[12:18]], 0)
    imag = jnp.concatenate([total[6:12], total[18:24]], 0)
    values = [(real[:, 128 * a : 128 * a + 128], imag[:, 128 * a : 128 * a + 128]) for a in range(8)]
    for k, pieces in enumerate(small_dft(values, -1)):
        windows[k // 2, 0:12, 256 * (k % 2) : 256 * (k % 2) + 256] = jnp.concatenate(pieces, 1)

    def inner(k, carry):
        table_copy(k).wait()
        high, low = split(parts[k])
        value = mul(table[k, 0], high) + mul(table[k, 1], high) + mul(table[k, 0], low)
        high, low = split(windows[k // 2, 0:12, pl.ds(pl.multiple_of(256 * (k % 2), 256), 256)])
        edge = mul_t(high, table[k, 0]) + mul_t(high, table[k, 1]) + mul_t(low, table[k, 0])
        for p in range(2):
            rows = edge[6 * p : 6 * p + 6]
            sides = [joined(rows[0:3, at : at + 128], rows[3:6, at : at + 128]) for at in (0, 128)]
            for half in range(2):
                for c in range(3):
                    for part in range(2):
                        row = 128 * part + 64 * half
                        to = 392 * p + 64 * (2 * c + part)
                        at = 128 * (3 * p + c)
                        out[2 * k + half, to : to + 64] = value[row : row + 64, at : at + 128]
                out[2 * k + half, 392 * p + 384 : 392 * p + 392] = jnp.concatenate(
                    [sides[part][half][c : c + 1] for c in range(3) for part in range(2)]
                    + [jnp.zeros((2, 128), F32)],
                    0,
                )
        return carry

    lax.fori_loop(0, 8, inner, 0)


def spectrum_kernel(
    meta, received, far_table, far_back, edge_table, edge_stack, far_spectrum, out, norm,
    spectrum, parts, back, edge_sum, table, table_back,
    spectrum_done, table_done, back_done,
):
    row = meta[64]

    def spectrum_copy(p, part):
        to = far_spectrum.at[part, :, pl.ds(2 * p, 2)]
        return pltpu.make_async_copy(spectrum.at[p, part], to, spectrum_done.at[2 * p + part])

    def table_copy(k):
        return pltpu.make_async_copy(far_table.at[k], table.at[k], table_done.at[k])

    def back_copy(k):
        return pltpu.make_async_copy(far_back.at[k], table_back.at[k], back_done.at[k])

    for k in range(8):
        table_copy(k).start()
        back_copy(k).start()

    index_y = 8 * (64 * (row % 2) + lax.broadcasted_iota(jnp.int32, (64, 128), 0)) + row // 2
    lane_x = lax.broadcasted_iota(jnp.int32, (64, 128), 1)
    wave_y = jnp.where(index_y < NY // 2, index_y, index_y - NY).astype(F32) * (TWO_PI / NY)
    sums = jnp.zeros((64, 128), F32)
    for p in range(2):
        base = 392 * p

        def outer(c, tile, carry):
            at = pl.multiple_of(tile * 8, 8)
            first = base + 128 * c
            values = [
                (received[s, pl.ds(first + at, 8)], received[s, pl.ds(first + 64 + at, 8)]) for s in range(16)
            ]
            for k, (real, imag) in enumerate(small_dft(values, -1)):
                to = 128 * (k // 8)
                first, second = joined(real, imag)
                parts[k % 8, pl.ds(128 * c + at, 8), to : to + 128] = first
                parts[k % 8, pl.ds(128 * c + 64 + at, 8), to : to + 128] = second
            return carry

        for c in range(3):
            lax.fori_loop(0, 8, functools.partial(outer, c), 0, unroll=8)
        columns = []
        for c in range(3):
            at = base + 384 + 2 * c
            rows = jnp.concatenate([received[s, at : at + 2] for s in range(16)], 0)
            high = rows.astype(BF16).astype(F32)
            columns.append(jnp.concatenate([high, rows - high, high, jnp.zeros((32, 128), F32)], 0).T.astype(BF16))
        edge = jnp.concatenate(columns, 0)
        edge_sum[...] = jnp.zeros_like(edge_sum)

        def inner(k, total):
            if p == 0:
                table_copy(k).wait()
                back_copy(k).wait()
            high, low = split(parts[k])
            value = mul(high, table[k, 0]) + mul(low, table[k, 0]) + mul(high, table[k, 1])
            value = value + mul(edge, edge_stack[k])
            index_x = 8 * lane_x + k
            wave_x = jnp.where(index_x < NX // 2, index_x, index_x - NX).astype(F32) * (TWO_PI / NX)
            flat = wave_x * wave_x + wave_y * wave_y
            valid = (index_y != NY // 2) & (index_x != NX // 2)
            to = pl.multiple_of(k * 128, 128)
            rows = [[None, None] for _ in range(3)]
            for h in range(2):
                index_z = 4 * meta[65] + 2 * p + h
                wave_z = index_z.astype(F32) * (TWO_PI / NZ)
                weight = jnp.where(index_z == 0, 1.0, 2.0).astype(F32) / CELLS
                squared = flat + wave_z * wave_z
                keep = valid & (squared > 0.0)
                inverse = jnp.where(keep, 1.0 / jnp.where(keep, squared, 1.0), 0.0)

                def crossed(vector, scale):
                    return [
                        (wave_y * vector[2] - wave_z * vector[1]) * scale,
                        (wave_z * vector[0] - wave_x * vector[2]) * scale,
                        (wave_x * vector[1] - wave_y * vector[0]) * scale,
                    ]

                start = [128 * c + 64 * h for c in range(3)]
                real = [value[s : s + 64, 0:128] for s in start]
                imag = [value[s : s + 64, 128:256] for s in start]
                grad_real = crossed(imag, -inverse)
                grad_imag = crossed(real, inverse)
                square = 0.0
                for c in range(3):
                    spectrum[p, 0, c, h, :, pl.ds(to, 128)] = grad_real[c]
                    spectrum[p, 1, c, h, :, pl.ds(to, 128)] = grad_imag[c]
                    square = square + grad_real[c] * grad_real[c] + grad_imag[c] * grad_imag[c]
                total = total + weight * square
                scale = inverse * weight
                back_real = crossed(grad_imag, -scale)
                back_imag = crossed(grad_real, scale)
                for c in range(3):
                    rows[c][h] = jnp.concatenate([back_real[c], back_imag[c]], 1)
            high, low = split(jnp.concatenate([rows[c][h] for c in range(3) for h in range(2)], 0))
            back[k] = mul(high, table_back[k, 0]) + mul(low, table_back[k, 0]) + mul(high, table_back[k, 1])
            edge_sum[...] += (
                mul_t(high, edge_table[k, 0]) + mul_t(high, edge_table[k, 1]) + mul_t(low, edge_table[k, 0])
            )
            return total

        sums = lax.fori_loop(0, 8, inner, sums, unroll=8)
        for part in range(2):
            spectrum_copy(p, part).start()

        def last(c, tile, carry):
            at = pl.multiple_of(tile * 8, 8)
            values = []
            for k in range(16):
                to = 128 * (k // 8)
                first = back[k % 8, pl.ds(128 * c + at, 8), to : to + 128]
                second = back[k % 8, pl.ds(128 * c + 64 + at, 8), to : to + 128]
                values.append(joined(first, second))
            for s, pieces in enumerate(small_dft(values, 1)):
                for part in range(2):
                    out[s, pl.ds(base + 128 * c + 64 * part + at, 8)] = pieces[part]
            return carry

        turned = [edge_sum[128 * c : 128 * c + 128, :].T for c in range(3)]
        for s in range(16):
            out[s, base + 384 : base + 392] = jnp.concatenate(
                [turned[c][2 * s : 2 * s + 2] for c in range(3)] + [jnp.zeros((2, 128), F32)], 0
            )
        for c in range(3):
            lax.fori_loop(0, 8, functools.partial(last, c), 0, unroll=8)
    norm[...] = jnp.sum(sums.reshape(8, 8, 128), axis=0)
    for p in range(2):
        for part in range(2):
            spectrum_copy(p, part).wait()


def gather_kernel(
    meta, points, depth, received, far_table, out, field_high, field_low, parts, edge, windows, table, table_done
):
    def table_copy(k):
        return pltpu.make_async_copy(far_table.at[k], table.at[k], table_done.at[k])

    for k in range(8):
        table_copy(k).start()

    def inner(k, carry):
        table_copy(k).wait()
        columns = []
        for p in range(2):
            for c in range(3):
                pieces = []
                for part in range(2):
                    for half in range(2):
                        at = 392 * p + 64 * (2 * c + part)
                        pieces.append(received[2 * k + half, at : at + 64])
                columns.append(jnp.concatenate(pieces, 0))
        high, low = split(jnp.concatenate(columns, 1))
        parts[k] = mul(table[k, 0], high) + mul(table[k, 1], high) + mul(table[k, 0], low)
        sides = []
        for p in range(2):
            at = 392 * p + 384
            sides.append(joined(received[2 * k, at : at + 8], received[2 * k + 1, at : at + 8]))
        rows = [
            jnp.concatenate(
                [sides[p][h][2 * c + part : 2 * c + part + 1] for p in range(2) for h in range(2) for c in range(3)],
                0,
            )
            for part in range(2)
        ]
        high, low = split(jnp.concatenate(rows, 1))
        edge[k] = mul_t(high, table[k, 0]) + mul_t(high, table[k, 1]) + mul_t(low, table[k, 0])
        return carry

    lax.fori_loop(0, 8, inner, 0)
    values = [(edge[k, :, 0:128], edge[k, :, 128:256]) for k in range(8)]
    planes = []
    for real, imag in small_dft(values, 1):
        planes.append(jnp.concatenate([real[0:6], imag[0:6], real[6:12], imag[6:12]], 0))
    plane = jnp.concatenate(planes, 1)
    for j in range(4):
        windows[j] = plane if j == 0 else pltpu.roll(plane, 1024 - 32 * j, 1)

    def outer(tile, carry):
        row = pl.multiple_of(tile * 16, 16)
        for c in range(3):
            for p in range(2):
                at = 128 * (3 * p + c)
                values = [
                    (parts[k, pl.ds(row, 16), at : at + 128], parts[k, pl.ds(128 + row, 16), at : at + 128])
                    for k in range(8)
                ]
                for a, pieces in enumerate(small_dft(values, 1)):
                    for part in range(2):
                        high, low = split(pieces[part])
                        lane = 256 * p + 128 * part
                        field_high[c, pl.ds(128 * a + row, 16), lane : lane + 128] = high
                        field_low[c, pl.ds(128 * a + row, 16), lane : lane + 128] = low
        return carry

    lax.fori_loop(0, 8, outer, 0)
    for c in range(3):
        field_high[c, 1024:1040, :] = field_high[c, 0:16, :]
        field_low[c, 1024:1040, :] = field_low[c, 0:16, :]

    def step(block, carry):
        place_x, place_y, _ = brick_place(meta[block])
        point = block_points(points, block)
        waves = depth[block]
        weight_high, weight_low = split(slab_weights(point, waves, place_x))
        along = hat(ramp((48, 128), 0) - point[1:2])
        row = pl.multiple_of(place_y * 32, 32)
        high = jnp.concatenate([field_high[c, pl.ds(row, 48), :] for c in range(3)], 0)
        low = jnp.concatenate([field_low[c, pl.ds(row, 48), :] for c in range(3)], 0)
        both = mul(high, jnp.concatenate([weight_high, weight_low], 1))
        value = both[:, :128] + both[:, 128:] + mul(low, weight_high)
        velocity = [jnp.sum(along * value[48 * c : 48 * c + 48], axis=0, keepdims=True) for c in range(3)]
        waves = edge_waves(point, waves, place_x)
        weight_high, weight_low = split(edge_weights(along))
        lane = pl.multiple_of(place_y // 4 * 128, 128)
        high, low = split(windows[place_y % 4, :, pl.ds(lane, 128)])
        value = mul(high, weight_high) + mul(low, weight_high) + mul(high, weight_low)
        more = sum(waves[i : i + 1] * value[3 * i : 3 * i + 3] for i in range(8))
        for c in range(3):
            out[block // 8, pl.ds(8 * c + block % 8, 1), :] = velocity[c] + more[c : c + 1]
        return carry

    lax.fori_loop(0, 64, step, 0, unroll=32)


def sums_kernel(counts, received, norms, velocity, out):
    row = lax.broadcasted_iota(jnp.int32, (8, 128), 0)
    count = jnp.zeros((8, 128), jnp.int32)
    for i in range(8):
        count = jnp.where(row == i, counts[i], count)
    live = lax.broadcasted_iota(jnp.int32, (8, 128), 1) < count
    square = jnp.zeros((8, 128), F32)
    for c in range(3):
        total = received[0, 8 * c : 8 * c + 8]
        for source in range(1, 8):
            total = total + received[source, 8 * c : 8 * c + 8]
        total = jnp.where(live, total, 0.0)
        square = square + total * total
        for i in range(8):
            velocity[c : c + 1, 128 * i : 128 * i + 128] = total[i : i + 1]
    norm = jnp.sum(norms[...], axis=0, keepdims=True)
    square = jnp.sum(square, axis=0, keepdims=True)
    tile = jnp.where(row == 0, norm, jnp.where(row == 1, square, 0.0))
    for dest in range(16):
        out[dest] = tile


def final_kernel(sums, residual, velocity, gradient, spectrum, out, values, loaded, stored):
    def load(i):
        source = gradient.at[i // 6, i // 2 % 3, pl.ds(i % 2 * 2, 2)]
        return pltpu.make_async_copy(source, values.at[i], loaded.at[i])

    def store(i):
        place = spectrum.at[i // 6, i // 2 % 3, pl.ds(i % 2 * 2, 2)]
        return pltpu.make_async_copy(values.at[i], place, stored.at[i])

    for i in range(12):
        load(i).start()
    total = jnp.sum(jnp.sum(sums[...], axis=0), axis=1, keepdims=True)
    length = total[0:1] / total[1:2]
    scale = length * (1.0 / math.sqrt(CELLS))
    for i in range(12):
        load(i).wait()
        values[i] = values[i] * scale
        store(i).start()
    out[...] = residual[...] - length * velocity[...]
    for i in range(12):
        store(i).wait()


def call(kernel, outs, specs, scratch=(), traffic=0, out_specs=VMEM, limit=VMEM_LIMIT):
    return pl.pallas_call(
        kernel,
        out_shape=outs,
        in_specs=specs,
        out_specs=out_specs,
        scratch_shapes=list(scratch),
        cost_estimate=pl.CostEstimate(flops=0, bytes_accessed=int(traffic), transcendentals=0),
        compiler_params=pltpu.CompilerParams(vmem_limit_bytes=limit),
    )


def near(value):
    return pltpu.with_memory_space_constraint(value, pltpu.VMEM)


def far(value):
    return pltpu.with_memory_space_constraint(value, pltpu.HBM)


def near_shape(*dims):
    return pltpu.VMEM(dims, F32)


def shape(*dims):
    return jax.ShapeDtypeStruct(dims, F32)


def spread_out(value, axis):
    count = lax.axis_size(axis)
    return lax.all_to_all(jnp.broadcast_to(value[None], (count,) + value.shape), axis, 0, 0, tiled=True)


def exchange(value):
    return lax.all_to_all(value, "row", 0, 0, tiled=True)


def body(offsets, measured, block_brick, block_count):
    row = lax.axis_index("row")
    col = lax.axis_index("col")
    packed, residual = call(
        pack_kernel, (shape(8, 8, 1024), shape(3, 1024)), [VMEM, VMEM, SMEM, SMEM], traffic=1e6, out_specs=(VMEM, VMEM)
    )(offsets, measured, block_brick, block_count)
    points = lax.all_to_all(packed, "col", 0, 0, tiled=True)
    bricks = points[:, 6, ::128].reshape(64).astype(jnp.int32)
    meta = jnp.concatenate([bricks, jnp.stack([row, col]).astype(jnp.int32)])
    y_table = table_y()
    x_table = table_x()
    forward_y = jnp.asarray(halves(y_table))
    inverse_y = jnp.asarray(halves(y_table.transpose(0, 2, 1)))
    forward_x = jnp.asarray(halves(x_table))
    inverse_x = jnp.asarray(halves(x_table.transpose(0, 2, 1)))

    edge_table = halves(table_edge())
    eight = pltpu.SemaphoreType.DMA((8,))
    sent, depth = call(
        spread_kernel,
        (near_shape(16, 784, 128), shape(64, 8, 128)),
        [SMEM, VMEM, ANY],
        [
            pltpu.VMEM((3, 1032, 512), F32),
            pltpu.VMEM((8, 256, 768), F32),
            pltpu.VMEM((4, 24, 1024), F32),
            TABLE,
            eight,
        ],
        40e6,
        (VMEM, VMEM),
        LIM_A,
    )(meta, points, forward_y)
    received = exchange(sent)
    spectrum, sent, norm = call(
        spectrum_kernel,
        (shape(2, 3, 4, 64, 1024), near_shape(16, 784, 128), shape(8, 128)),
        [SMEM, VMEM, ANY, ANY, VMEM, VMEM],
        [
            pltpu.VMEM((2, 2, 3, 2, 64, 1024), F32),
            pltpu.VMEM((8, 384, 256), F32),
            pltpu.VMEM((8, 384, 256), F32),
            pltpu.VMEM((384, 128), F32),
            TABLE,
            TABLE,
            pltpu.SemaphoreType.DMA((4,)),
            eight,
            eight,
        ],
        40e6,
        (ANY, VMEM, VMEM),
        LIM_X,
    )(meta, near(received), forward_x, inverse_x, jnp.asarray(edge_table), jnp.asarray(stacked(edge_table)))
    received = exchange(sent)
    velocity = call(
        gather_kernel,
        shape(8, 24, 128),
        [SMEM, VMEM, VMEM, VMEM, ANY],
        [
            pltpu.VMEM((3, 1040, 512), BF16),
            pltpu.VMEM((3, 1040, 512), BF16),
            pltpu.VMEM((8, 256, 768), F32),
            pltpu.VMEM((8, 12, 256), F32),
            pltpu.VMEM((4, 24, 1024), F32),
            TABLE,
            eight,
        ],
        40e6,
        VMEM,
        LIM_A,
    )(meta, points, depth, near(received), inverse_y)
    velocity = lax.all_to_all(velocity, "col", 0, 0, tiled=True)
    velocity, sums = call(sums_kernel, (shape(3, 1024), shape(16, 8, 128)), [SMEM] + [VMEM] * 2, traffic=1e6, out_specs=(VMEM, VMEM))(
        block_count, velocity, norm
    )
    sums = lax.all_to_all(sums, "row", 0, 0, tiled=True)
    sums = spread_out(jnp.sum(sums, axis=0), "col")
    twelve = pltpu.SemaphoreType.DMA((12,))
    return call(
        final_kernel,
        (shape(2, 3, 4, 64, 1024), shape(3, 1024)),
        [VMEM, VMEM, VMEM, ANY],
        [pltpu.VMEM((12, 2, 64, 1024), F32), twelve, twelve],
        13e6,
        (ANY, VMEM),
    )(sums, residual, velocity, spectrum)


def solution(mesh):
    in_specs = (
        P(None, ("row", "col")),
        P(None, ("row", "col")),
        P(("row", "col")),
        P(("row", "col")),
    )
    out_specs = (P(None, None, "col", "row", None), P(None, ("row", "col")))
    return jax.shard_map(body, mesh=mesh, in_specs=in_specs, out_specs=out_specs, check_vma=False)
```
